32 devices in a mesh: rep: 2 (over x), seq: 16 (over z, y, core).
Axes of the slice: x: 2, y: 2, z: 4, core: 2. Of those that a mesh axis runs over, the one named last changes fastest.
Arguments:
- cached_keys: bfloat16 [32768, 1024], P(('rep', 'seq')), parts along dimension 0, may hold values from -6 to 6
- cached_values: bfloat16 [32768, 1024], P(('rep', 'seq')), parts along dimension 0, may hold values from -6 to 6
- window_queries: bfloat16 [256, 8192], P(('rep', 'seq')), parts along dimension 0
- kept_count: int32 [32], P(('rep', 'seq')), parts along dimension 0, may hold values from 1 to 640, 8192 in all
- kept_entry: int32 [20480], P(('rep', 'seq')), parts along dimension 0, may hold values from 0 to 8191
- row_owner: int32 [20480], P(('rep', 'seq')), parts along dimension 0, may hold values from 0 to 15, as said below
Outputs:
- importance: float32 [16, 16384], P('rep', 'seq'), parts along dimension 0
- compact_rows: bfloat16 [20480, 256], P(('rep', 'seq')), parts along dimension 0
- compact_score: bfloat16 [20480], P(('rep', 'seq')), parts along dimension 0
The draws below stay inside these ranges and needn't reach their ends.
There are 2 independent parts, one for each index of `rep`. The reference program is written for one: setup_inputs(seed, part) draws one part's arguments, and reference() takes and returns one part's arrays. A program takes and returns all parts, laid end to end along the dimension named above; each array names one. Nothing has to cross between parts.
Inputs may be any that keep to these rules, and one draw needn't show every extreme that they name: `kept_count`: the counts of the 16 devices sum to 8192. `kept_entry`: entries may repeat. `row_owner`: among the 640 slots of one device every owner is named by exactly 40 slots.
All inputs are finite; a program needn't handle non-finite values.
Results may differ from the reference program's by a relative error of at most 0.0004.
Values may be sent and summed in bfloat16 or wider, within the bound.
No kernel may reach another device: no remote copies, remote signals or barrier semaphores. Data moves between devices by JAX's collectives and lax.ppermute only.
A program may use at most 64 MiB of HBM per device.

```python
import math
import jax
import jax.numpy as jnp
import numpy as np
from jax import lax

HEADS = 64
KV_HEADS = 8
HEAD_DIM = 128
GROUP = 8
WINDOW = 128
POOL = 7
TOK_DEV = 1024
SEQ = 16384
SLOTS = 640
CAP = 40
KEPT = 8192
N_SEQ = 16


def draw_cached_keys(key, part):
    return jnp.clip(jax.random.normal(jax.random.fold_in(key, 3), (SEQ, KV_HEADS * HEAD_DIM), jnp.float32), -6.0, 6.0).astype(jnp.bfloat16)


def draw_window_queries(key, part):
    return jnp.clip(jax.random.normal(jax.random.fold_in(key, 5), (WINDOW, HEADS * HEAD_DIM), jnp.float32), -6.0, 6.0).astype(jnp.bfloat16)


def draw_row_owner(key, part):
    peers = N_SEQ
    filled = jnp.tile(jnp.arange(peers, dtype=jnp.int32)[None, :], (peers, CAP))
    shuffle = jax.random.randint(jax.random.fold_in(key, 23), (peers, SLOTS), 0, 2 ** 19) * SLOTS + jnp.arange(SLOTS)[None, :]
    order = jnp.argsort(shuffle, axis=1, stable=True)
    return jnp.take_along_axis(filled, order, axis=1).reshape(-1).astype(jnp.int32)


def set_ends(values, own_key, smallest, top_value):
    longest = values.shape.index(max(values.shape))
    spots = []
    for shift in (0, 1):
        where = [jax.random.randint(jax.random.fold_in(own_key, axis), (), 0, length) for axis, length in enumerate(values.shape)]
        where[longest] = (where[longest] + shift) % values.shape[longest]
        spots.append(tuple(where))
    return values.at[spots[0]].set(smallest).at[spots[1]].set(top_value)


def levels(key, shape, pieces, low, largest):
    gain, own = 1.0, jax.random.fold_in(key, 6)
    for position, blocks in pieces:
        steps = jnp.exp(jax.random.uniform(jax.random.fold_in(own, position), (blocks,), jnp.float32, low / len(pieces), largest / len(pieces)))
        gain = gain * jnp.repeat(steps, shape[position] // blocks).reshape([-1 if axis == position else 1 for axis in range(len(shape))])
    return gain


def split_up(amount, total, bound, slope):
    portions = [(1 << 20) // math.isqrt(standing ** slope) + 1 for standing in range(2, amount + 1)]
    spare, given = total - bound - (amount - 1), [1] * (amount - 1)
    while spare > 0:
        candidates = [i for i in range(amount - 1) if given[i] < bound]
        pool, remaining = sum([portions[i] for i in candidates]), spare
        for i in candidates:
            addition = min(bound - given[i], max(1, remaining * portions[i] // pool), spare)
            given[i] = given[i] + addition
            spare = spare - addition
    return np.array([bound] + given)


def ragged_sizes(rng, number_of, total, most, slope):
    if number_of == 2:
        one = jax.random.randint(rng, (), max(1, total - most), min(most, total - 1) + 1)
        return jnp.stack([one, total - one])
    sizes = jnp.asarray(split_up(number_of, total, most, slope), jnp.int32)
    twos = (number_of - 1) // 2
    giver, sink = sizes[1:1 + 2 * twos:2], sizes[2:2 + 2 * twos:2]
    room = jnp.minimum(giver - 1, most - sink)
    moved = jax.random.randint(jax.random.fold_in(rng, 1), (twos,), 0, 1 << 20) % (room + 1)
    sizes = sizes.at[1:1 + 2 * twos:2].set(giver - moved).at[2:2 + 2 * twos:2].set(sink + moved)
    return sizes[jax.random.permutation(jax.random.fold_in(rng, 2), number_of)]


def bell_draw(rng, dims, spread, most, shards=(), kind=jnp.bfloat16):
    loudness = levels(rng, dims, shards, -0.22, 0.18) if shards else 1.0
    result = jax.random.normal(rng, dims, jnp.float32) * spread * loudness
    return jnp.minimum(jnp.maximum(result, -most), most).astype(kind)


def setup_inputs(seed: int = 0, part: int = 0) -> dict:
    splits = jax.random.split(jax.random.key(seed), 7)
    part_splits = jax.random.split(jax.random.fold_in(splits[6], part), 7)
    return {
        "cached_keys": draw_cached_keys(jax.random.fold_in(jax.random.fold_in(splits[6], part), 71), part),
        "cached_values": bell_draw(part_splits[1], (SEQ, KV_HEADS * HEAD_DIM), 1.0, 6.0, ((0, 16),)),
        "window_queries": draw_window_queries(jax.random.fold_in(jax.random.fold_in(splits[6], part), 71), part),
        "kept_count": ragged_sizes(part_splits[3], N_SEQ, KEPT, SLOTS, 2).astype(jnp.int32),
        "kept_entry": set_ends(jax.random.randint(part_splits[4], (N_SEQ * SLOTS,), 0, KV_HEADS * TOK_DEV), jax.random.fold_in(part_splits[4], 1), 0, (KV_HEADS * TOK_DEV) - 1).astype(jnp.int32),
        "row_owner": draw_row_owner(jax.random.fold_in(jax.random.fold_in(splits[6], part), 71), part),
    }


def window_groups(window_queries):
    shaped = window_queries.reshape(WINDOW, KV_HEADS, GROUP, HEAD_DIM).transpose(1, 2, 0, 3)
    return shaped.reshape(KV_HEADS, GROUP * WINDOW, HEAD_DIM).astype(jnp.float32)


def block_scores(query_groups, key_block):
    return jnp.einsum("gqd,gtd->gqt", query_groups, key_block.astype(jnp.float32)) * (HEAD_DIM ** -0.5)


def reference(cached_keys, cached_values, window_queries, kept_count, kept_entry, row_owner):
    query_groups = window_groups(window_queries)
    key_blocks = cached_keys.reshape(N_SEQ, TOK_DEV, KV_HEADS, HEAD_DIM).transpose(0, 2, 1, 3)

    def stat_step(carry, key_block):
        run_peak, run_total = carry
        scores = block_scores(query_groups, key_block)
        new_peak = jnp.maximum(run_peak, jnp.max(scores, axis=2))
        run_total = run_total * jnp.exp(run_peak - new_peak) + jnp.sum(jnp.exp(scores - new_peak[:, :, None]), axis=2)
        return (new_peak, run_total), None

    initial = (jnp.full((KV_HEADS, GROUP * WINDOW), -jnp.inf, jnp.float32), jnp.zeros((KV_HEADS, GROUP * WINDOW), jnp.float32))
    (glob_peak, glob_total), _ = lax.scan(stat_step, initial, key_blocks)
    inverse = 1.0 / glob_total

    def mass_step(carry, key_block):
        scores = block_scores(query_groups, key_block)
        return carry, jnp.sum(jnp.exp(scores - glob_peak[:, :, None]) * inverse[:, :, None], axis=1)

    _, column_mass = lax.scan(mass_step, jnp.zeros((), jnp.float32), key_blocks)
    column_mass = column_mass.transpose(1, 0, 2).reshape(KV_HEADS, SEQ)
    margin = POOL // 2
    padded = jnp.pad(column_mass, ((0, 0), (margin, margin)))
    pooled = padded[:, 0:SEQ]
    for offset in range(1, POOL):
        pooled = pooled + padded[:, offset:offset + SEQ]
    importance = pooled * (SEQ / (GROUP * WINDOW * POOL))

    everything = jnp.arange(N_SEQ * SLOTS, dtype=jnp.int32)
    device = everything // SLOTS
    within = everything % SLOTS
    is_live = within < kept_count[device]
    member = ((row_owner[:, None] == jnp.arange(N_SEQ, dtype=jnp.int32)[None, :]) & is_live[:, None]).astype(jnp.int32)
    member = member.reshape(N_SEQ, SLOTS, N_SEQ)
    earlier = jnp.cumsum(member, axis=1) - member
    slot_rank = jnp.sum(earlier * member, axis=2).reshape(-1)
    head_index = kept_entry // TOK_DEV
    token_index = device * TOK_DEV + kept_entry % TOK_DEV
    row_index = token_index * KV_HEADS + head_index
    key_rows = cached_keys.reshape(SEQ * KV_HEADS, HEAD_DIM)[row_index]
    value_rows = cached_values.reshape(SEQ * KV_HEADS, HEAD_DIM)[row_index]
    payload = jnp.concatenate([key_rows, value_rows], axis=1)
    score_rows = importance[head_index, token_index].astype(jnp.bfloat16)
    total_rows = N_SEQ * N_SEQ * CAP
    target = jnp.where(is_live, row_owner * (N_SEQ * CAP) + device * CAP + slot_rank, total_rows)
    compact_rows = jnp.zeros((total_rows, 2 * HEAD_DIM), jnp.bfloat16).at[target].set(payload, mode="drop")
    compact_score = jnp.zeros((total_rows,), jnp.bfloat16).at[target].set(score_rows, mode="drop")
    return importance, compact_rows, compact_score
```

```python
import functools

import jax
import jax.numpy as jnp
from jax import lax
from jax.experimental import pallas as pl
from jax.experimental.pallas import tpu as pltpu
from jax.sharding import PartitionSpec as P

HEADS = 64
KV_HEADS = 8
HEAD_DIM = 128
GROUP = 8
WINDOW = 128
POOL = 7
HALF = KV_HEADS // 2
EDGE = 16
SCALE2 = HEAD_DIM ** (-0.5) * 1.4426950408889634
MIB = 1 << 20

VMEM = pl.BlockSpec(memory_space=pltpu.VMEM)
SMEM = pl.BlockSpec(memory_space=pltpu.SMEM)


def nt(a, b, precision=None):
    return lax.dot_general(
        a, b, (((1,), (1,)), ((), ())), precision=precision, preferred_element_type=jnp.float32
    )


def one_hot(mask):
    return jnp.where(mask, 1.0, 0.0).astype(jnp.bfloat16)


def iota(shape, dim):
    return lax.broadcasted_iota(jnp.int32, shape, dim)


def compact_kernel(peers, count_ref, entry_ref, owner_ref, k_ref, v_ref, rows_ref, code_ref):
    positions = k_ref.shape[0]
    slots = entry_ref.shape[1]
    capacity = slots // peers
    owner, entry = owner_ref[...], entry_ref[...]
    live = iota((1, slots), 1) < count_ref[0]
    member = jnp.where((owner == iota((peers, slots), 0)) & live, 1.0, 0.0)
    before = one_hot(iota((slots, slots), 0) < iota((slots, slots), 1))
    earlier = jnp.dot(member.astype(jnp.bfloat16), before, preferred_element_type=jnp.float32)
    rank = jnp.sum(earlier * member, axis=0, keepdims=True).astype(jnp.int32)
    target = jnp.where(live, owner * capacity + rank, -1)
    placed = one_hot(iota((slots, slots), 0) == target)
    token, head = entry % positions, entry // positions
    line = iota((8, slots), 0)
    facts = jnp.where(
        line == 0, 1, jnp.where(line == 1, head, jnp.where(line == 2, token // 64, token % 64))
    )
    facts = facts.astype(jnp.float32).astype(jnp.bfloat16)
    by_row = nt(facts, placed)
    row_token = jnp.where(by_row[0:1] > 0.5, by_row[2:3] * 64 + by_row[3:4], -1.0)
    code_ref[...] = jnp.where(iota((8, slots), 0) == 0, row_token, by_row[1:2])
    by_col = nt(placed, facts)
    col_head = by_col[:, 1:2].astype(jnp.int32)
    col_token = jnp.where(by_col[:, 0:1] > 0.5, by_col[:, 2:3] * 64 + by_col[:, 3:4], -1.0)
    col_token = col_token.astype(jnp.int32)
    step = 128 if slots % 128 == 0 else slots
    for start in range(0, slots, step):
        token_part = col_token[start : start + step]
        head_part = col_head[start : start + step]
        pick = one_hot(iota((step, positions), 1) == token_part)
        for side, source in enumerate((k_ref, v_ref)):
            found = jnp.dot(pick, source[...], preferred_element_type=jnp.float32)
            kept = jnp.zeros((step, HEAD_DIM), jnp.float32)
            for g in range(KV_HEADS):
                part = found[:, g * HEAD_DIM : (g + 1) * HEAD_DIM]
                kept = kept + jnp.where(head_part == g, part, 0.0)
            rows_ref[start : start + step, side * HEAD_DIM : (side + 1) * HEAD_DIM] = kept.astype(
                jnp.bfloat16
            )


def query_rows(block_refs, g):
    parts = []
    for ref in block_refs:
        for h in range(GROUP):
            first = (g * GROUP + h) * HEAD_DIM
            parts.append(ref[:, first : first + HEAD_DIM])
    return jnp.concatenate(parts, axis=0)


def local_stats(block_refs, k_refs, store):
    per_block = GROUP * block_refs[0].shape[0]
    for g in range(HALF):
        rows = query_rows(block_refs, g)
        count = rows.shape[0]
        peak = jnp.full((1, count), -jnp.inf, jnp.float32)
        total = jnp.zeros((1, count), jnp.float32)
        for k_ref in k_refs:
            tokens = k_ref.shape[0]
            step = min(512, tokens)
            for start in range(0, tokens, step):
                keys = k_ref[start : start + step, g * HEAD_DIM : (g + 1) * HEAD_DIM]
                scores = nt(keys, rows)
                higher = jnp.maximum(peak, jnp.max(scores, axis=0, keepdims=True))
                total = total * jnp.exp2((peak - higher) * SCALE2) + jnp.sum(
                    jnp.exp2((scores - higher) * SCALE2), axis=0, keepdims=True
                )
                peak = higher
        lse = peak * SCALE2 + jnp.log2(total)
        for b in range(len(block_refs)):
            store(b, g, lse[:, b * per_block : (b + 1) * per_block])


def sender(chip, offset):
    return 0 if offset is None else chip ^ offset


def early_stats_kernel(count, *refs):
    blocks, (k_own, k_sib), out_ref = refs[:count], refs[count : count + 2], refs[-1]

    def store(b, g, lse):
        out_ref[b, g : g + 1, :] = lse

    local_stats(blocks, (k_own, k_sib), store)


def stats_kernel(offsets, early, dests, *refs):
    place_ref, refs = refs[0], refs[1:]
    if early:
        early_ref, refs = refs[0], refs[1:]
    late = len(offsets) - early
    blocks, (k_own, k_sib), out_ref, hold = (
        refs[:late], refs[late : late + 2], refs[late + 2], refs[late + 3])
    chip = place_ref[0] // 2

    for b in range(early):
        hold[sender(chip, offsets[b])] = early_ref[b]

    def store(b, g, lse):
        hold[sender(chip, offsets[early + b]), g : g + 1, :] = lse

    local_stats(blocks, (k_own, k_sib), store)
    everything = hold[...]
    for d in range(dests):
        out_ref[d] = everything


def split3(x):
    high = x.astype(jnp.bfloat16)
    rest = x - high.astype(jnp.float32)
    middle = rest.astype(jnp.bfloat16)
    low = (rest - middle.astype(jnp.float32)).astype(jnp.bfloat16)
    return high, middle, low


def mass_kernel(offsets, peers, factor, *refs):
    place_ref, stats_ref, code_own_ref, code_sib_ref = refs[:4]
    blocks = refs[4 : 4 + len(offsets)]
    k_own, k_sib, edge_own, edge_sib, imp_own, imp_sib, score_ref, lse_ref = refs[4 + len(offsets) :]
    tokens = k_own.shape[0]
    core = place_ref[0] % 2
    chip = place_ref[0] // 2
    chips = peers // 2
    is_low = core == 0

    stats = stats_ref[...]
    top = jnp.max(stats, axis=0)
    lse_ref[...] = top + jnp.log2(jnp.sum(jnp.exp2(stats - top[None]), axis=0))

    ones = jnp.ones((8, HEAD_DIM), jnp.float32)
    masses = []
    for which, (k_ref, first_col) in enumerate(
        ((k_own, None), (k_sib, None), (edge_own, core), (edge_sib, core))
    ):
        found = []
        for g in range(HALF):
            rows = query_rows(blocks, g)
            lse = jnp.concatenate(
                [lse_ref[sender(chip, off), g : g + 1, :] for off in offsets], axis=1
            )
            step = min(512, k_ref.shape[0])
            for start in range(0, k_ref.shape[0], step):
                cols = slice(g * HEAD_DIM, (g + 1) * HEAD_DIM)
                if first_col is None:
                    keys = k_ref[start : start + step, cols]
                else:
                    low = k_ref[start : start + step, cols]
                    high = k_ref[
                        start : start + step,
                        (HALF + g) * HEAD_DIM : (HALF + g + 1) * HEAD_DIM,
                    ]
                    keys = jnp.where(is_low, low, high)
                weights = jnp.exp2(nt(keys, rows) * SCALE2 - lse)
                folded = weights[:, 0:HEAD_DIM]
                for first in range(HEAD_DIM, weights.shape[1], HEAD_DIM):
                    folded = folded + weights[:, first : first + HEAD_DIM]
                found.append(nt(ones, folded, lax.Precision.HIGHEST)[0:1])
        per_head = len(found) // HALF
        masses.append(
            jnp.concatenate(
                [jnp.concatenate(found[g * per_head : (g + 1) * per_head], axis=1) for g in range(HALF)],
                axis=0,
            )
        )
    own, sib, rim_own, rim_sib = masses
    first = jnp.where(is_low, own, sib)
    second = jnp.where(is_low, sib, own)
    before = jnp.where(is_low, rim_own, rim_sib)[:, EDGE - POOL // 2 :]
    after = jnp.where(is_low, rim_sib, rim_own)[:, : POOL // 2]
    before = jnp.where(chip == 0, 0.0, before)
    after = jnp.where(chip == chips - 1, 0.0, after)
    padded = jnp.concatenate([before, first, second, after], axis=1)
    pooled = padded[:, 0 : 2 * tokens]
    for shift in range(1, POOL):
        pooled = pooled + padded[:, shift : shift + 2 * tokens]
    importance = pooled * factor
    halves = (importance[:, :tokens], importance[:, tokens:])
    imp_own[...] = jnp.where(is_low, halves[0], halves[1])
    imp_sib[...] = jnp.where(is_low, halves[1], halves[0])
    slots = code_own_ref.shape[1]
    capacity = slots // peers
    for side in range(2):
        code = jnp.where(core == side, code_own_ref[...], code_sib_ref[...]).astype(jnp.int32)
        parts = jnp.concatenate(split3(halves[side]), axis=0)
        pick = one_hot(iota((tokens, slots), 0) == code[0:1])
        hits = jnp.dot(parts, pick, preferred_element_type=jnp.float32)
        value = hits[0:HALF] + hits[HALF : 2 * HALF] + hits[2 * HALF : 3 * HALF]
        mine = iota((HALF, slots), 0) + core * HALF == code[1:2]
        score = jnp.sum(jnp.where(mine, value, 0.0), axis=0, keepdims=True)
        for p in range(peers):
            score_ref[p, side : side + 1, 0:capacity] = score[:, p * capacity : (p + 1) * capacity]


def per_device(cached_keys, cached_values, window_queries, kept_count, kept_entry, row_owner):
    positions = cached_keys.shape[0]
    peers = lax.axis_size("seq")
    chips = peers // 2
    slots = kept_entry.shape[0]
    capacity = slots // peers
    me = lax.axis_index("seq")
    core = me % 2
    place = me.astype(jnp.int32).reshape(1)
    half_keys = HALF * HEAD_DIM
    half_queries = HALF * GROUP * HEAD_DIM

    def swap(x, distance):
        return lax.ppermute(x, "seq", [(i, i ^ distance) for i in range(peers)])

    def half(x, which, width):
        return lax.dynamic_slice_in_dim(x, which * width, width, axis=1)

    sibling_queries = swap(window_queries, 1)
    piece = jnp.concatenate(
        [half(window_queries, core, half_queries), half(sibling_queries, core, half_queries)], axis=0
    )
    lines = chips // 2
    if piece.shape[0] % 16 == 0 and chips % 2 == 0 and lines & (lines - 1) == 0:
        far = [swap(piece, 4 * d) for d in range(1, lines)]
        near = [piece, swap(piece, 2)]
        across = swap(jnp.concatenate(far, axis=0), 2)
        rows = piece.shape[0]
        blocks = near + far + [across[i * rows : (i + 1) * rows] for i in range(lines - 1)]
        offsets = [0, 1] + [2 * d for d in range(1, lines)] + [2 * d + 1 for d in range(1, lines)]
        early = 1 + lines
    else:
        same_core = [[i for i in range(peers) if i % 2 == c] for c in range(2)]
        blocks = [lax.all_gather(piece, "seq", axis=0, tiled=True, axis_index_groups=same_core)]
        offsets, early = [None], 0
    count = len(blocks)

    k_own = half(cached_keys, core, half_keys)
    k_sib = swap(half(cached_keys, 1 - core, half_keys), 1)
    rim = jnp.where(core == 1, cached_keys[positions - EDGE :], cached_keys[:EDGE])
    ring = [(2 * i + 1, 2 * i + 2) for i in range(chips - 1)]
    edge_own = lax.ppermute(rim, "seq", ring + [(b, a) for a, b in ring])
    edge_sib = swap(edge_own, 1)

    rows_out, code_own = pl.pallas_call(
        functools.partial(compact_kernel, peers),
        out_shape=(
            jax.ShapeDtypeStruct((slots, 2 * HEAD_DIM), jnp.bfloat16),
            jax.ShapeDtypeStruct((8, slots), jnp.float32),
        ),
        in_specs=[SMEM, VMEM, VMEM, VMEM, VMEM],
        out_specs=(VMEM, VMEM),
        compiler_params=pltpu.CompilerParams(vmem_limit_bytes=32 * MIB),
        name="compact",
    )(kept_count, kept_entry.reshape(1, slots), row_owner.reshape(1, slots), cached_keys, cached_values)
    code_sib = swap(code_own, 1)
    got_rows = lax.all_to_all(
        rows_out.reshape(peers, capacity, 2 * HEAD_DIM), "seq", split_axis=0, concat_axis=0, tiled=True
    )

    per_block = GROUP * blocks[0].shape[0]
    first = []
    if early:
        first = [
            pl.pallas_call(
                functools.partial(early_stats_kernel, early),
                out_shape=jax.ShapeDtypeStruct((early, HALF, per_block), jnp.float32),
                in_specs=[VMEM] * (early + 2),
                out_specs=VMEM,
                compiler_params=pltpu.CompilerParams(vmem_limit_bytes=32 * MIB),
                name="early_stats",
            )(*blocks[:early], k_own, k_sib)
        ]
    sent = pl.pallas_call(
        functools.partial(stats_kernel, offsets, early, chips),
        out_shape=jax.ShapeDtypeStruct((chips, count, HALF, per_block), jnp.float32),
        in_specs=[SMEM] + [VMEM] * (len(first) + count - early + 2),
        out_specs=VMEM,
        scratch_shapes=[pltpu.VMEM((count, HALF, per_block), jnp.float32)],
        compiler_params=pltpu.CompilerParams(vmem_limit_bytes=32 * MIB),
        name="late_stats",
    )(place, *first, *blocks[early:], k_own, k_sib)
    stats = lax.all_to_all(
        sent,
        "seq",
        split_axis=0,
        concat_axis=0,
        tiled=True,
        axis_index_groups=[[i for i in range(peers) if i % 2 == c] for c in range(2)],
    )

    factor = peers * positions / (GROUP * WINDOW * POOL)
    imp_own, imp_sib, score = pl.pallas_call(
        functools.partial(mass_kernel, offsets, peers, factor),
        out_shape=(
            jax.ShapeDtypeStruct((HALF, positions), jnp.float32),
            jax.ShapeDtypeStruct((HALF, positions), jnp.float32),
            jax.ShapeDtypeStruct((peers, 2, 128), jnp.float32),
        ),
        in_specs=[SMEM] + [VMEM] * (7 + count),
        out_specs=(VMEM, VMEM, VMEM),
        scratch_shapes=[pltpu.VMEM((count, HALF, per_block), jnp.float32)],
        compiler_params=pltpu.CompilerParams(vmem_limit_bytes=48 * MIB),
        name="mass",
    )(place, stats, code_own, code_sib, *blocks, k_own, k_sib, edge_own, edge_sib)

    got_score = lax.all_to_all(score, "seq", split_axis=0, concat_axis=0, tiled=True)
    by_core = got_score.reshape(chips, 2, 2, 128)[..., :capacity]
    score_out = (by_core[:, 0] + by_core[:, 1]).astype(jnp.bfloat16)
    imp_other = swap(imp_sib, 1)
    importance = jnp.where(
        core == 0,
        jnp.concatenate([imp_own, imp_other], axis=0),
        jnp.concatenate([imp_other, imp_own], axis=0),
    )
    return (
        importance,
        got_rows.reshape(peers * capacity, 2 * HEAD_DIM),
        score_out.reshape(peers * capacity),
    )


def solution(mesh):
    in_specs = (
        P(("rep", "seq"), None),
        P(("rep", "seq"), None),
        P(("rep", "seq"), None),
        P(("rep", "seq")),
        P(("rep", "seq")),
        P(("rep", "seq")),
    )
    out_specs = (P("rep", "seq"), P(("rep", "seq"), None), P(("rep", "seq")))
    return jax.shard_map(
        per_device, mesh=mesh, in_specs=in_specs, out_specs=out_specs, check_vma=False
    )
```

```python
import functools

import jax
import jax.numpy as jnp
from jax import lax
from jax.experimental import pallas as pl
from jax.experimental.pallas import tpu as pltpu
from jax.sharding import PartitionSpec as P

HEADS = 64
KV_HEADS = 8
HEAD_DIM = 128
GROUP = 8
WINDOW = 128
POOL = 7
HALF = KV_HEADS // 2
EDGE = 16
SCALE2 = HEAD_DIM ** (-0.5) * 1.4426950408889634
MIB = 1 << 20

VMEM = pl.BlockSpec(memory_space=pltpu.VMEM)
SMEM = pl.BlockSpec(memory_space=pltpu.SMEM)
ANYWHERE = pl.BlockSpec(memory_space=pl.ANY)
GRANT = 56 * MIB


def nt(a, b, precision=None):
    return lax.dot_general(
        a, b, (((1,), (1,)), ((), ())), precision=precision, preferred_element_type=jnp.float32
    )


def one_hot(mask):
    return jnp.where(mask, 1.0, 0.0).astype(jnp.bfloat16)


def iota(shape, dim):
    return lax.broadcasted_iota(jnp.int32, shape, dim)


def compact_kernel(
    peers, count_ref, entry_ref, owner_ref, k_source, v_source, rows_ref, code_ref, k_ref, v_ref, sems
):
    copies = (
        pltpu.make_async_copy(k_source, k_ref, sems.at[0]),
        pltpu.make_async_copy(v_source, v_ref, sems.at[1]),
    )
    for copy in copies:
        copy.start()
    positions = k_ref.shape[0]
    slots = entry_ref.shape[1]
    capacity = slots // peers
    owner, entry = owner_ref[...], entry_ref[...]
    live = iota((1, slots), 1) < count_ref[0]
    member = jnp.where((owner == iota((peers, slots), 0)) & live, 1.0, 0.0)
    before = one_hot(iota((slots, slots), 0) < iota((slots, slots), 1))
    earlier = jnp.dot(member.astype(jnp.bfloat16), before, preferred_element_type=jnp.float32)
    rank = jnp.sum(earlier * member, axis=0, keepdims=True).astype(jnp.int32)
    target = jnp.where(live, owner * capacity + rank, -1)
    placed = one_hot(iota((slots, slots), 0) == target)
    token, head = entry % positions, entry // positions
    line = iota((8, slots), 0)
    facts = jnp.where(
        line == 0, 1, jnp.where(line == 1, head, jnp.where(line == 2, token // 64, token % 64))
    )
    facts = facts.astype(jnp.float32).astype(jnp.bfloat16)
    by_row = nt(facts, placed)
    row_token = jnp.where(by_row[0:1] > 0.5, by_row[2:3] * 64 + by_row[3:4], -1.0)
    code_ref[...] = jnp.where(iota((8, slots), 0) == 0, row_token, by_row[1:2])
    by_col = nt(placed, facts)
    col_head = by_col[:, 1:2].astype(jnp.int32)
    col_token = jnp.where(by_col[:, 0:1] > 0.5, by_col[:, 2:3] * 64 + by_col[:, 3:4], -1.0)
    col_token = col_token.astype(jnp.int32)
    step = 128 if slots % 128 == 0 else slots
    for side, source in enumerate((k_ref, v_ref)):
        copies[side].wait()
        for start in range(0, slots, step):
            token_part = col_token[start : start + step]
            head_part = col_head[start : start + step]
            pick = one_hot(iota((step, positions), 1) == token_part)
            found = jnp.dot(pick, source[...], preferred_element_type=jnp.float32)
            kept = jnp.zeros((step, HEAD_DIM), jnp.float32)
            for g in range(KV_HEADS):
                part = found[:, g * HEAD_DIM : (g + 1) * HEAD_DIM]
                kept = kept + jnp.where(head_part == g, part, 0.0)
            rows_ref[start : start + step, side * HEAD_DIM : (side + 1) * HEAD_DIM] = kept.astype(
                jnp.bfloat16
            )


def query_rows(block_refs, g):
    parts = []
    for ref in block_refs:
        for h in range(GROUP):
            first = (g * GROUP + h) * HEAD_DIM
            parts.append(ref[:, first : first + HEAD_DIM])
    return jnp.concatenate(parts, axis=0)


def spread(limits, value):
    low, high = limits
    return jnp.minimum(low, jnp.min(value)), jnp.maximum(high, jnp.max(value))


def fetch_keys(sources, held, sems):
    copies = []
    for g in range(HALF):
        for i, source in enumerate(sources):
            cols = slice(g * HEAD_DIM, (g + 1) * HEAD_DIM)
            copies.append(pltpu.make_async_copy(source.at[:, cols], held.at[g, i], sems.at[g, i]))
    for copy in copies:
        copy.start()

    def wait(g):
        for copy in copies[2 * g : 2 * g + 2]:
            copy.wait()

    return wait


def local_stats(block_refs, k_refs, store):
    per_block = GROUP * block_refs[0].shape[0]
    tokens = k_refs[0].shape[0]

    def keep(g, lse):
        for b in range(len(block_refs)):
            store(b, g, lse[:, b * per_block : (b + 1) * per_block])

    limits = (jnp.float32(jnp.inf), jnp.float32(-jnp.inf))
    step = min(512, tokens)
    for g in range(HALF):
        rows = query_rows(block_refs, g)
        count = rows.shape[0]
        total = jnp.zeros((8, count), jnp.float32)
        cols = slice(g * HEAD_DIM, (g + 1) * HEAD_DIM)
        for k_ref in k_refs:
            for start in range(0, tokens, step):
                weights = jnp.exp2(nt(k_ref[start : start + step, cols], rows) * SCALE2)
                total = total + jnp.sum(weights.reshape(step // 8, 8, count), axis=0)
        total = jnp.sum(total, axis=0, keepdims=True)
        limits = spread(limits, total)
        keep(g, jnp.log2(total))

    in_range = (limits[0] > 2.0**-60) & (limits[1] < 2.0**100)

    @pl.when(jnp.logical_not(in_range))
    def _():
        part = min(256, tokens)
        for g in range(HALF):
            rows = query_rows(block_refs, g)
            count = rows.shape[0]
            carry = (jnp.full((1, count), -jnp.inf, jnp.float32), jnp.zeros((1, count), jnp.float32))
            cols = slice(g * HEAD_DIM, (g + 1) * HEAD_DIM)
            for k_ref in k_refs:

                def advance(j, carry):
                    peak, total = carry
                    start = pl.multiple_of(j * part, part)
                    scores = nt(k_ref[pl.ds(start, part), cols], rows)
                    higher = jnp.maximum(peak, jnp.max(scores, axis=0, keepdims=True))
                    total = total * jnp.exp2((peak - higher) * SCALE2) + jnp.sum(
                        jnp.exp2((scores - higher) * SCALE2), axis=0, keepdims=True
                    )
                    return higher, total

                carry = lax.fori_loop(0, tokens // part, advance, carry)
            keep(g, carry[0] * SCALE2 + jnp.log2(carry[1]))


def sender(chip, offset):
    return 0 if offset is None else chip ^ offset


def fetch(sources, held, sems):
    copies = [pltpu.make_async_copy(x, held.at[i], sems.at[i]) for i, x in enumerate(sources)]
    for copy in copies:
        copy.start()
    return copies


def early_stats_kernel(count, *refs):
    blocks, k_refs, out_ref = refs[:count], refs[count : count + 2], refs[-1]

    def store(b, g, lse):
        out_ref[b, g : g + 1, :] = lse

    local_stats(blocks, k_refs, store)


def stats_kernel(offsets, early, dests, *refs):
    place_ref, k_refs = refs[0], refs[1:3]
    out_ref, hold = refs[-2:]
    chip = place_ref[0] // 2
    done = 0
    for ref, size in zip(refs[3:], early):
        for b in range(size):
            hold[sender(chip, offsets[done + b])] = ref[b]
        done += size

    def store(b, g, lse):
        hold[sender(chip, offsets[done + b]), g : g + 1, :] = lse

    local_stats(refs[3 + len(early) : -2], k_refs, store)
    everything = hold[...]
    for d in range(dests):
        out_ref[d] = everything


def fetch(sources, held, sems):
    copies = [pltpu.make_async_copy(x, held.at[i], sems.at[i]) for i, x in enumerate(sources)]
    for copy in copies:
        copy.start()
    return copies


def split3(x):
    high = x.astype(jnp.bfloat16)
    rest = x - high.astype(jnp.float32)
    middle = rest.astype(jnp.bfloat16)
    low = (rest - middle.astype(jnp.float32)).astype(jnp.bfloat16)
    return high, middle, low


def mass_kernel(offsets, peers, factor, width, edges, *refs):
    count = len(offsets)
    place_ref, stats_ref, k_own, k_sib = refs[:4]
    code_sources = refs[4:6]
    edge_refs, refs = refs[6 : 6 + edges], refs[6 + edges :]
    sources = refs[:count]
    imp_own, imp_sib, score_ref = refs[count : count + 3]
    lse_ref, side_ref, blocks_held, held, codes, block_sems, sems, code_sems = refs[count + 3 :]
    copies = fetch(sources, blocks_held, block_sems)
    wait = fetch_keys((k_own, k_sib), held, sems)
    code_copies = fetch(code_sources, codes, code_sems)
    blocks = [blocks_held.at[i] for i in range(count)]
    tokens = held.shape[2]
    core = place_ref[0] % 2
    chip = place_ref[0] // 2
    chips = peers // 2
    is_low = core == 0

    stats = stats_ref[...]
    top = jnp.max(stats, axis=0)
    lse_ref[...] = top + jnp.log2(jnp.sum(jnp.exp2(stats - top[None]), axis=0))

    for copy in copies:
        copy.wait()
    step = min(512, tokens)
    found = [[], []]
    rims = []
    for g in range(HALF):
        rows = query_rows(blocks, g)
        lse = jnp.concatenate([lse_ref[sender(chip, off), g : g + 1, :] for off in offsets], axis=1)
        parts = jnp.concatenate(
            split3(lse) + (jnp.zeros((5, lse.shape[1]), jnp.bfloat16),), axis=0
        )
        side_ref[...] = lax.dot_general(
            parts, jnp.ones((8, HEAD_DIM), jnp.bfloat16), (((0,), (0,)), ((), ())),
            preferred_element_type=jnp.float32,
        )
        wait(g)
        for i in range(2):
            line = []
            for start in range(0, tokens, step):
                shift = jnp.concatenate([side_ref[...]] * (step // HEAD_DIM), axis=1)
                weights = jnp.exp2(nt(rows, held[g, i, start : start + step, :]) * SCALE2 - shift)
                line.append(jnp.sum(weights, axis=0, keepdims=True))
            found[i].append(jnp.concatenate(line, axis=1))
        if edges:
            low = slice(g * HEAD_DIM, (g + 1) * HEAD_DIM)
            high = slice((HALF + g) * HEAD_DIM, (HALF + g + 1) * HEAD_DIM)
            rim_keys = [jnp.where(is_low, ref[:, low], ref[:, high]) for ref in edge_refs]
        else:
            cols = slice(width + g * HEAD_DIM, width + (g + 1) * HEAD_DIM)
            rim_keys = []
            for other in (chip ^ jnp.maximum(chip - 1, 0), chip ^ jnp.minimum(chip + 1, chips - 1)):
                where = sum(jnp.where(other == off, i, 0) for i, off in enumerate(offsets))
                rim_keys.append(blocks_held[where, :, cols])
        weights = jnp.exp2(nt(jnp.concatenate(rim_keys, axis=0), rows) * SCALE2 - lse)
        folded = weights[:, 0:HEAD_DIM]
        for first in range(HEAD_DIM, weights.shape[1], HEAD_DIM):
            folded = folded + weights[:, first : first + HEAD_DIM]
        rims.append(jnp.sum(folded.T, axis=0, keepdims=True))
    own = jnp.concatenate(found[0], axis=0)
    sib = jnp.concatenate(found[1], axis=0)
    rim = jnp.concatenate(rims, axis=0)
    first = jnp.where(is_low, own, sib)
    second = jnp.where(is_low, sib, own)
    side = POOL // 2
    if edges:
        rim_own, rim_sib = rim[:, :EDGE], rim[:, EDGE : 2 * EDGE]
        before = jnp.where(is_low, rim_own, rim_sib)[:, EDGE - side :]
        after = jnp.where(is_low, rim_sib, rim_own)[:, :side]
    else:
        size = blocks_held.shape[1]
        mid = size // 2
        before = jnp.where(is_low, rim[:, size - side : size], rim[:, mid - side : mid])
        after = jnp.where(is_low, rim[:, size : size + side], rim[:, size + mid : size + mid + side])
    before = jnp.where(chip == 0, 0.0, before)
    after = jnp.where(chip == chips - 1, 0.0, after)
    padded = jnp.concatenate([before, first, second, after], axis=1)
    pooled = padded[:, 0 : 2 * tokens]
    for shift in range(1, POOL):
        pooled = pooled + padded[:, shift : shift + 2 * tokens]
    importance = pooled * factor
    halves = (importance[:, :tokens], importance[:, tokens:])
    imp_own[...] = jnp.where(is_low, halves[0], halves[1])
    imp_sib[...] = jnp.where(is_low, halves[1], halves[0])
    for copy in code_copies:
        copy.wait()
    slots = codes.shape[2]
    capacity = slots // peers
    for side in range(2):
        code = jnp.where(core == side, codes[0], codes[1]).astype(jnp.int32)
        parts = jnp.concatenate(split3(halves[side]), axis=0)
        pick = one_hot(iota((tokens, slots), 0) == code[0:1])
        hits = jnp.dot(parts, pick, preferred_element_type=jnp.float32)
        value = hits[0:HALF] + hits[HALF : 2 * HALF] + hits[2 * HALF : 3 * HALF]
        mine = iota((HALF, slots), 0) + core * HALF == code[1:2]
        score = jnp.sum(jnp.where(mine, value, 0.0), axis=0, keepdims=True)
        for p in range(peers):
            score_ref[p, side : side + 1, 0:capacity] = score[:, p * capacity : (p + 1) * capacity]


def after(x, *earlier):
    return lax.optimization_barrier((x, earlier))[0]


def per_device(cached_keys, cached_values, window_queries, kept_count, kept_entry, row_owner):
    positions = cached_keys.shape[0]
    peers = lax.axis_size("seq")
    chips = peers // 2
    slots = kept_entry.shape[0]
    capacity = slots // peers
    me = lax.axis_index("seq")
    core = me % 2
    place = me.astype(jnp.int32).reshape(1)
    half_keys = HALF * HEAD_DIM
    half_queries = HALF * GROUP * HEAD_DIM

    def swap(x, distance):
        return lax.ppermute(x, "seq", [(i, i ^ distance) for i in range(peers)])

    def half(x, which, width):
        return lax.dynamic_slice_in_dim(x, which * width, width, axis=1)

    def joined(parts):
        return jnp.concatenate(parts, axis=0)

    lines = chips // 2
    shard_rows = window_queries.shape[0]
    stepwise = shard_rows % 8 == 0 and chips % 4 == 0 and lines & (lines - 1) == 0
    edge = shard_rows if stepwise else EDGE
    rim = jnp.where(core == 1, cached_keys[positions - edge :], cached_keys[:edge])
    sibling_queries = swap(window_queries, 1)
    pair = [half(window_queries, core, half_queries), half(sibling_queries, core, half_queries)]
    if stepwise:
        sibling_rim = swap(rim, 1)
        ends = [half(rim, core, half_keys), half(sibling_rim, core, half_keys)]
        piece = joined([jnp.concatenate(x, axis=1) for x in zip(pair, ends)])
        edges = []
    else:
        piece = joined(pair)
        offsets = [None]
        ring = [(2 * i + 1, 2 * i + 2) for i in range(chips - 1)]
        edge_own = lax.ppermute(rim, "seq", ring + [(b, a) for a, b in ring])
        edges = [edge_own, swap(edge_own, 1)]

    def keys_held():
        return [
            pltpu.VMEM((HALF, 2, positions, HEAD_DIM), jnp.bfloat16),
            pltpu.SemaphoreType.DMA((HALF, 2)),
        ]

    def blocks_held(some):
        return [
            pltpu.VMEM((len(some),) + some[0].shape, jnp.bfloat16),
            pltpu.SemaphoreType.DMA((len(some),)),
        ]

    def score_cost(some):
        queries = len(some) * HALF * GROUP * some[0].shape[0]
        return pl.CostEstimate(
            flops=4 * queries * positions * HEAD_DIM,
            bytes_accessed=2 * positions * half_keys,
            transcendentals=0,
        )

    def early_stats(some):
        shape = (len(some), HALF, GROUP * some[0].shape[0])
        return pl.pallas_call(
            functools.partial(early_stats_kernel, len(some)),
            out_shape=jax.ShapeDtypeStruct(shape, jnp.float32),
            in_specs=[VMEM] * (len(some) + 2),
            out_specs=VMEM,
            compiler_params=pltpu.CompilerParams(vmem_limit_bytes=8 * MIB),
            cost_estimate=score_cost(some),
            name="early_stats",
        )(*some, k_own, k_sib)

    if stepwise:
        line, distance = [(0, piece)], lines // 2
        while distance:
            for off, block in list(line):
                if distance == 1 and off == 0:
                    near = swap(block, 4)
                    line.append((2, near))
                else:
                    if distance == 1:
                        block = after(block, near)
                    line.append((off ^ 2 * distance, swap(block, 4 * distance)))
            distance //= 2
        beside = {off: swap(block, 2) for off, block in line[:-1]}
        start = [(0, piece), (1, beside[0]), (2, near), (3, beside[2])]
        sets = [start]
        for off, block in line[:-1]:
            if off not in (0, 2):
                sets.append([(off, block), (off ^ 1, beside[off])])
        final = line[-1]
        ready_keys = after(cached_keys, piece)
    else:
        same_core = [[i for i in range(peers) if i % 2 == c] for c in range(2)]
        gathered = lax.all_gather(piece, "seq", axis=0, tiled=True, axis_index_groups=same_core)
        sets, final = [], (None, gathered)
        ready_keys = after(cached_keys, piece)

    k_own = half(ready_keys, core, half_keys)
    k_sib = swap(half(ready_keys, 1 - core, half_keys), 1)

    first = [early_stats([block for _, block in some]) for some in sets]
    if stepwise:
        off, block = final
        sets.append([final, (off ^ 1, swap(after(block, beside[2]), 2))])
    else:
        sets.append([final])
    blocks = [block for some in sets for _, block in some]
    offsets = [off for some in sets for off, _ in some]
    late = [block for _, block in sets[-1]]
    count = len(offsets)
    per_block = GROUP * blocks[0].shape[0]
    sent = pl.pallas_call(
        functools.partial(stats_kernel, offsets, [x.shape[0] for x in first], chips),
        out_shape=jax.ShapeDtypeStruct((chips, count, HALF, per_block), jnp.float32),
        in_specs=[SMEM] + [VMEM] * (2 + len(first) + len(late)),
        out_specs=VMEM,
        scratch_shapes=[pltpu.VMEM((count, HALF, per_block), jnp.float32)],
        compiler_params=pltpu.CompilerParams(vmem_limit_bytes=8 * MIB),
        cost_estimate=score_cost(late),
        name="late_stats",
    )(place, k_own, k_sib, *first, *late)

    rows_out, code_own = pl.pallas_call(
        functools.partial(compact_kernel, peers),
        out_shape=(
            jax.ShapeDtypeStruct((slots, 2 * HEAD_DIM), jnp.bfloat16),
            jax.ShapeDtypeStruct((8, slots), jnp.float32),
        ),
        in_specs=[SMEM, VMEM, VMEM, ANYWHERE, ANYWHERE],
        out_specs=(VMEM, VMEM),
        scratch_shapes=[
            pltpu.VMEM(cached_keys.shape, jnp.bfloat16),
            pltpu.VMEM(cached_values.shape, jnp.bfloat16),
            pltpu.SemaphoreType.DMA((2,)),
        ],
        compiler_params=pltpu.CompilerParams(vmem_limit_bytes=GRANT),
        cost_estimate=pl.CostEstimate(
            flops=4 * slots * positions * KV_HEADS * HEAD_DIM,
            bytes_accessed=4 * positions * KV_HEADS * HEAD_DIM,
            transcendentals=0,
        ),
        name="compact",
    )(
        kept_count,
        after(kept_entry, sent).reshape(1, slots),
        row_owner.reshape(1, slots),
        cached_keys,
        cached_values,
    )
    code_sib = swap(code_own, 1)
    got_rows = lax.all_to_all(
        rows_out.reshape(peers, capacity, 2 * HEAD_DIM), "seq", split_axis=0, concat_axis=0, tiled=True
    ).reshape(slots, 2 * HEAD_DIM)

    stats = lax.all_to_all(
        sent,
        "seq",
        split_axis=0,
        concat_axis=0,
        tiled=True,
        axis_index_groups=[[i for i in range(peers) if i % 2 == c] for c in range(2)],
    )
    factor = peers * positions / (GROUP * WINDOW * POOL)
    imp_own, imp_sib, score = pl.pallas_call(
        functools.partial(mass_kernel, offsets, peers, factor, half_queries, len(edges)),
        out_shape=(
            jax.ShapeDtypeStruct((HALF, positions), jnp.float32),
            jax.ShapeDtypeStruct((HALF, positions), jnp.float32),
            jax.ShapeDtypeStruct((peers, 2, 128), jnp.float32),
        ),
        in_specs=[SMEM, VMEM] + [ANYWHERE] * 4 + [VMEM] * len(edges) + [ANYWHERE] * count,
        out_specs=(VMEM, VMEM, VMEM),
        scratch_shapes=[
            pltpu.VMEM((count, HALF, per_block), jnp.float32),
            pltpu.VMEM((count * per_block, HEAD_DIM), jnp.float32),
            blocks_held(blocks)[0],
            keys_held()[0],
            pltpu.VMEM((2, 8, slots), jnp.float32),
            blocks_held(blocks)[1],
            keys_held()[1],
            pltpu.SemaphoreType.DMA((2,)),
        ],
        compiler_params=pltpu.CompilerParams(vmem_limit_bytes=GRANT),
        cost_estimate=score_cost(blocks),
        name="mass",
    )(place, stats, k_own, k_sib, code_own, code_sib, *edges, *blocks)

    got_score = lax.all_to_all(after(score, got_rows), "seq", split_axis=0, concat_axis=0, tiled=True)
    by_core = got_score.reshape(chips, 2, 2, 128)[..., :capacity]
    score_out = (by_core[:, 0] + by_core[:, 1]).astype(jnp.bfloat16)
    imp_other = swap(imp_sib, 1)
    importance = jnp.where(
        core == 0,
        jnp.concatenate([imp_own, imp_other], axis=0),
        jnp.concatenate([imp_other, imp_own], axis=0),
    )
    return (
        importance,
        got_rows,
        score_out.reshape(peers * capacity),
    )


def solution(mesh):
    in_specs = (
        P(("rep", "seq"), None),
        P(("rep", "seq"), None),
        P(("rep", "seq"), None),
        P(("rep", "seq")),
        P(("rep", "seq")),
        P(("rep", "seq")),
    )
    out_specs = (P("rep", "seq"), P(("rep", "seq"), None), P(("rep", "seq")))
    return jax.shard_map(
        per_device, mesh=mesh, in_specs=in_specs, out_specs=out_specs, check_vma=False
    )
```

```python
import functools

import jax
import jax.numpy as jnp
from jax import lax
from jax.experimental import pallas as pl
from jax.experimental.pallas import tpu as pltpu
from jax.sharding import PartitionSpec as P

HEADS = 64
KV_HEADS = 8
HEAD_DIM = 128
GROUP = 8
WINDOW = 128
POOL = 7
HALF = KV_HEADS // 2
EDGE = 16
SCALE2 = HEAD_DIM ** (-0.5) * 1.4426950408889634
MIB = 1 << 20

VMEM = pl.BlockSpec(memory_space=pltpu.VMEM)
SMEM = pl.BlockSpec(memory_space=pltpu.SMEM)
ANYWHERE = pl.BlockSpec(memory_space=pl.ANY)
GRANT = 56 * MIB


def nt(a, b, precision=None):
    return lax.dot_general(
        a, b, (((1,), (1,)), ((), ())), precision=precision, preferred_element_type=jnp.float32
    )


def one_hot(mask):
    return jnp.where(mask, 1.0, 0.0).astype(jnp.bfloat16)


def iota(shape, dim):
    return lax.broadcasted_iota(jnp.int32, shape, dim)


def codes_kernel(positions, peers, own_ref, sib_ref, own_code_ref, sib_code_ref, column_ref):
    for mine, ref, code_ref in ((True, own_ref, own_code_ref), (False, sib_ref, sib_code_ref)):
        slots = ref.shape[1]
        entry, owner, count = ref[0:1], ref[1:2], ref[2:3]
        capacity = slots // peers
        live = iota((1, slots), 1) < count
        member = jnp.where((owner == iota((peers, slots), 0)) & live, 1.0, 0.0)
        before = one_hot(iota((slots, slots), 0) < iota((slots, slots), 1))
        earlier = jnp.dot(member.astype(jnp.bfloat16), before, preferred_element_type=jnp.float32)
        rank = jnp.sum(earlier * member, axis=0, keepdims=True).astype(jnp.int32)
        target = jnp.where(live, owner * capacity + rank, -1)
        placed = one_hot(iota((slots, slots), 0) == target)
        token, head = entry % positions, entry // positions
        line = iota((8, slots), 0)
        facts = jnp.where(
            line == 0, 1, jnp.where(line == 1, head, jnp.where(line == 2, token // 64, token % 64))
        )
        facts = facts.astype(jnp.float32).astype(jnp.bfloat16)
        by_row = nt(facts, placed)
        row_token = jnp.where(by_row[0:1] > 0.5, by_row[2:3] * 64 + by_row[3:4], -1.0)
        code_ref[...] = jnp.where(line == 0, row_token, by_row[1:2])
        if mine:
            by_col = nt(placed, facts)
            col_token = jnp.where(by_col[:, 0:1] > 0.5, by_col[:, 2:3] * 64 + by_col[:, 3:4], -1.0)
            column = jnp.where(iota((slots, 8), 1) == 0, col_token, by_col[:, 1:2])
            column_ref[...] = column


def compact_kernel(column_ref, k_source, v_source, packed_ref, k_ref, v_ref, rows_ref, sems):
    copies = (
        pltpu.make_async_copy(k_source, k_ref, sems.at[0]),
        pltpu.make_async_copy(v_source, v_ref, sems.at[1]),
    )
    for copy in copies:
        copy.start()
    positions = k_ref.shape[0]
    slots = rows_ref.shape[0]
    token = column_ref[:, 0:1].astype(jnp.int32)
    head = column_ref[:, 1:2].astype(jnp.int32)
    pick = one_hot(iota((slots, positions), 1) == token)
    for side, source in enumerate((k_ref, v_ref)):
        copies[side].wait()
        kept = jnp.zeros((slots, HEAD_DIM), jnp.float32)
        for g in range(0, KV_HEADS, 2):
            pair = source[:, g * HEAD_DIM : (g + 2) * HEAD_DIM]
            found = jnp.dot(pick, pair, preferred_element_type=jnp.float32)
            kept = kept + jnp.where(head == g, found[:, :HEAD_DIM], 0.0)
            kept = kept + jnp.where(head == g + 1, found[:, HEAD_DIM:], 0.0)
        rows_ref[:, side * HEAD_DIM : (side + 1) * HEAD_DIM] = kept
    peers, room, width = packed_ref.shape
    capacity = slots // peers
    rest = jnp.zeros((room - capacity, width), jnp.float32)
    for p in range(peers):
        rows = rows_ref[p * capacity : (p + 1) * capacity, :]
        packed_ref[p] = jnp.concatenate([rows, rest], axis=0).astype(jnp.bfloat16)


def query_rows(block_refs, g):
    parts = []
    for ref in block_refs:
        for h in range(GROUP):
            first = (g * GROUP + h) * HEAD_DIM
            parts.append(ref[:, first : first + HEAD_DIM])
    return jnp.concatenate(parts, axis=0)


def spread(limits, value):
    low, high = limits
    return jnp.minimum(low, jnp.min(value)), jnp.maximum(high, jnp.max(value))


def local_stats(block_refs, k_refs, store):
    per_block = GROUP * block_refs[0].shape[0]
    tokens = k_refs[0].shape[0]

    def keep(g, lse):
        for b in range(len(block_refs)):
            store(b, g, lse[:, b * per_block : (b + 1) * per_block])

    limits = (jnp.float32(jnp.inf), jnp.float32(-jnp.inf))
    step = min(512, tokens)
    for g in range(HALF):
        rows = query_rows(block_refs, g)
        count = rows.shape[0]
        total = jnp.zeros((8, count), jnp.float32)
        cols = slice(g * HEAD_DIM, (g + 1) * HEAD_DIM)
        for k_ref in k_refs:
            for start in range(0, tokens, step):
                weights = jnp.exp2(nt(k_ref[start : start + step, cols], rows) * SCALE2)
                total = total + jnp.sum(weights.reshape(step // 8, 8, count), axis=0)
        total = jnp.sum(total, axis=0, keepdims=True)
        limits = spread(limits, total)
        keep(g, jnp.log2(total))

    in_range = (limits[0] > 2.0**-60) & (limits[1] < 2.0**100)

    @pl.when(jnp.logical_not(in_range))
    def _():
        part = min(256, tokens)
        for g in range(HALF):
            rows = query_rows(block_refs, g)
            count = rows.shape[0]
            carry = (jnp.full((1, count), -jnp.inf, jnp.float32), jnp.zeros((1, count), jnp.float32))
            cols = slice(g * HEAD_DIM, (g + 1) * HEAD_DIM)
            for k_ref in k_refs:

                def advance(j, carry):
                    peak, total = carry
                    start = pl.multiple_of(j * part, part)
                    scores = nt(k_ref[pl.ds(start, part), cols], rows)
                    higher = jnp.maximum(peak, jnp.max(scores, axis=0, keepdims=True))
                    total = total * jnp.exp2((peak - higher) * SCALE2) + jnp.sum(
                        jnp.exp2((scores - higher) * SCALE2), axis=0, keepdims=True
                    )
                    return higher, total

                carry = lax.fori_loop(0, tokens // part, advance, carry)
            keep(g, carry[0] * SCALE2 + jnp.log2(carry[1]))


def sender(chip, offset):
    return 0 if offset is None else chip ^ offset


def early_stats_kernel(count, *refs):
    blocks, k_refs, out_ref = refs[:count], refs[count : count + 2], refs[-1]

    def store(b, g, lse):
        out_ref[b, g : g + 1, :] = lse

    local_stats(blocks, k_refs, store)


def stats_kernel(offsets, early, dests, *refs):
    place_ref, k_refs = refs[0], refs[1:3]
    out_ref, hold = refs[-2:]
    chip = place_ref[0] // 2
    done = 0
    for ref, size in zip(refs[3:], early):
        for b in range(size):
            hold[sender(chip, offsets[done + b])] = ref[b]
        done += size

    def store(b, g, lse):
        hold[sender(chip, offsets[done + b]), g : g + 1, :] = lse

    local_stats(refs[3 + len(early) : -2], k_refs, store)
    everything = hold[...]
    for d in range(dests):
        out_ref[d] = everything


def split3(x):
    high = x.astype(jnp.bfloat16)
    rest = x - high.astype(jnp.float32)
    middle = rest.astype(jnp.bfloat16)
    low = (rest - middle.astype(jnp.float32)).astype(jnp.bfloat16)
    return high, middle, low


def mass_kernel(offsets, peers, factor, width, edges, score_row, *refs):
    count = len(offsets)
    place_ref, stats_ref, k_own, k_sib = refs[:4]
    codes, packed_ref = refs[4:6], refs[6]
    edge_refs, refs = refs[7 : 7 + edges], refs[7 + edges :]
    blocks = refs[:count]
    imp_own, imp_sib, out_ref, lse_ref, side_ref, sem = refs[count:]
    copy = pltpu.make_async_copy(packed_ref, out_ref, sem)
    copy.start()
    tokens = k_own.shape[0]
    core = place_ref[0] % 2
    chip = place_ref[0] // 2
    chips = peers // 2
    is_low = core == 0

    stats = stats_ref[...]
    top = jnp.max(stats, axis=0)
    lse_ref[...] = top + jnp.log2(jnp.sum(jnp.exp2(stats - top[None]), axis=0))

    step = min(512, tokens)
    found = [[], []]
    rims = []
    for g in range(HALF):
        rows = query_rows(blocks, g)
        lse = jnp.concatenate([lse_ref[sender(chip, off), g : g + 1, :] for off in offsets], axis=1)
        parts = jnp.concatenate(
            split3(lse) + (jnp.zeros((5, lse.shape[1]), jnp.bfloat16),), axis=0
        )
        side_ref[...] = lax.dot_general(
            parts, jnp.ones((8, HEAD_DIM), jnp.bfloat16), (((0,), (0,)), ((), ())),
            preferred_element_type=jnp.float32,
        )
        cols = slice(g * HEAD_DIM, (g + 1) * HEAD_DIM)
        for i, k_ref in enumerate((k_own, k_sib)):
            line = []
            for start in range(0, tokens, step):
                shift = jnp.concatenate([side_ref[...]] * (step // HEAD_DIM), axis=1)
                weights = jnp.exp2(nt(rows, k_ref[start : start + step, cols]) * SCALE2 - shift)
                line.append(jnp.sum(weights, axis=0, keepdims=True))
            found[i].append(jnp.concatenate(line, axis=1))
        if edges:
            low = slice(g * HEAD_DIM, (g + 1) * HEAD_DIM)
            high = slice((HALF + g) * HEAD_DIM, (HALF + g + 1) * HEAD_DIM)
            rim_keys = [jnp.where(is_low, ref[:, low], ref[:, high]) for ref in edge_refs]
        else:
            cols = slice(width + g * HEAD_DIM, width + (g + 1) * HEAD_DIM)
            rim_keys = []
            for other in (chip ^ jnp.maximum(chip - 1, 0), chip ^ jnp.minimum(chip + 1, chips - 1)):
                found_keys = blocks[0][:, cols]
                for off, ref in zip(offsets[1:], blocks[1:]):
                    found_keys = jnp.where(other == off, ref[:, cols], found_keys)
                rim_keys.append(found_keys)
        weights = jnp.exp2(nt(jnp.concatenate(rim_keys, axis=0), rows) * SCALE2 - lse)
        folded = weights[:, 0:HEAD_DIM]
        for first in range(HEAD_DIM, weights.shape[1], HEAD_DIM):
            folded = folded + weights[:, first : first + HEAD_DIM]
        rims.append(jnp.sum(folded.T, axis=0, keepdims=True))
    own = jnp.concatenate(found[0], axis=0)
    sib = jnp.concatenate(found[1], axis=0)
    rim = jnp.concatenate(rims, axis=0)
    first = jnp.where(is_low, own, sib)
    second = jnp.where(is_low, sib, own)
    side = POOL // 2
    if edges:
        rim_own, rim_sib = rim[:, :EDGE], rim[:, EDGE : 2 * EDGE]
        before = jnp.where(is_low, rim_own, rim_sib)[:, EDGE - side :]
        after = jnp.where(is_low, rim_sib, rim_own)[:, :side]
    else:
        size = blocks[0].shape[0]
        mid = size // 2
        before = jnp.where(is_low, rim[:, size - side : size], rim[:, mid - side : mid])
        after = jnp.where(is_low, rim[:, size : size + side], rim[:, size + mid : size + mid + side])
    before = jnp.where(chip == 0, 0.0, before)
    after = jnp.where(chip == chips - 1, 0.0, after)
    padded = jnp.concatenate([before, first, second, after], axis=1)
    pooled = padded[:, 0 : 2 * tokens]
    for shift in range(1, POOL):
        pooled = pooled + padded[:, shift : shift + 2 * tokens]
    importance = pooled * factor
    halves = (importance[:, :tokens], importance[:, tokens:])
    imp_own[...] = jnp.where(is_low, halves[0], halves[1])
    imp_sib[...] = jnp.where(is_low, halves[1], halves[0])
    slots = codes[0].shape[1]
    capacity = slots // peers
    scores = []
    for side in range(2):
        code = jnp.where(core == side, codes[0][...], codes[1][...]).astype(jnp.int32)
        parts = jnp.concatenate(split3(halves[side]), axis=0)
        pick = one_hot(iota((tokens, slots), 0) == code[0:1])
        hits = jnp.dot(parts, pick, preferred_element_type=jnp.float32)
        value = hits[0:HALF] + hits[HALF : 2 * HALF] + hits[2 * HALF : 3 * HALF]
        mine = iota((HALF, slots), 0) + core * HALF == code[1:2]
        scores.append(jnp.sum(jnp.where(mine, value, 0.0), axis=0, keepdims=True))
    both = jnp.concatenate(scores + [jnp.zeros((6, slots), jnp.float32)], axis=0)
    copy.wait()
    for p in range(peers):
        out_ref[p, score_row : score_row + 8, 0:capacity] = both[
            :, p * capacity : (p + 1) * capacity
        ].astype(jnp.bfloat16)


def after(x, *earlier):
    return lax.optimization_barrier((x, earlier))[0]


def per_device(cached_keys, cached_values, window_queries, kept_count, kept_entry, row_owner):
    positions = cached_keys.shape[0]
    peers = lax.axis_size("seq")
    chips = peers // 2
    slots = kept_entry.shape[0]
    capacity = slots // peers
    me = lax.axis_index("seq")
    core = me % 2
    place = me.astype(jnp.int32).reshape(1)
    half_keys = HALF * HEAD_DIM
    half_queries = HALF * GROUP * HEAD_DIM

    def swap(x, distance):
        return lax.ppermute(x, "seq", [(i, i ^ distance) for i in range(peers)])

    def half(x, which, width):
        return lax.dynamic_slice_in_dim(x, which * width, width, axis=1)

    def joined(parts):
        return jnp.concatenate(parts, axis=0)

    sibling_queries = swap(window_queries, 1)
    own_queries = half(window_queries, core, half_queries)
    ready_keys = after(cached_keys, sibling_queries)
    k_own = half(ready_keys, core, half_keys)
    k_other = half(ready_keys, 1 - core, half_keys)
    k_sib = swap(k_other, 1)

    lines = chips // 2
    shard_rows = window_queries.shape[0]
    stepwise = shard_rows % 8 == 0 and chips % 4 == 0 and lines & (lines - 1) == 0
    edge = shard_rows if stepwise else EDGE
    rim = jnp.where(core == 1, cached_keys[positions - edge :], cached_keys[:edge])
    pair = [own_queries, half(sibling_queries, core, half_queries)]
    if stepwise:
        sibling_rim = swap(rim, 1)
        ends = [half(rim, core, half_keys), half(sibling_rim, core, half_keys)]
        piece = joined([jnp.concatenate(x, axis=1) for x in zip(pair, ends)])
        edges = []
    else:
        piece = joined(pair)
        offsets = [None]
        ring = [(2 * i + 1, 2 * i + 2) for i in range(chips - 1)]
        edge_own = lax.ppermute(rim, "seq", ring + [(b, a) for a, b in ring])
        edges = [edge_own, swap(edge_own, 1)]

    def score_cost(some):
        queries = len(some) * HALF * GROUP * some[0].shape[0]
        return pl.CostEstimate(
            flops=4 * queries * positions * HEAD_DIM,
            bytes_accessed=2 * positions * half_keys,
            transcendentals=0,
        )

    def early_stats(some):
        shape = (len(some), HALF, GROUP * some[0].shape[0])
        return pl.pallas_call(
            functools.partial(early_stats_kernel, len(some)),
            out_shape=jax.ShapeDtypeStruct(shape, jnp.float32),
            in_specs=[VMEM] * (len(some) + 2),
            out_specs=VMEM,
            compiler_params=pltpu.CompilerParams(vmem_limit_bytes=8 * MIB),
            cost_estimate=score_cost(some),
            name="early_stats",
        )(*some, k_own, k_sib)

    if stepwise:
        line, distance = [(0, piece)], lines // 2
        beside = {0: swap(piece, 2)}
        while distance:
            for off, block in list(line):
                if distance == 1 and off == 0:
                    near = swap(block, 4)
                    line.append((2, near))
                else:
                    if distance == 1:
                        block = after(block, near, beside[0])
                    line.append((off ^ 2 * distance, swap(block, 4 * distance)))
            distance //= 2
        beside.update({off: swap(block, 2) for off, block in line[1:-1]})
        start = [(0, piece), (1, beside[0]), (2, near), (3, beside[2])]
        sets = [start]
        for off, block in line[:-1]:
            if off not in (0, 2):
                sets.append([(off, block), (off ^ 1, beside[off])])
        final = line[-1]
        arrived = (line[1][1], near, beside[0])
    else:
        same_core = [[i for i in range(peers) if i % 2 == c] for c in range(2)]
        gathered = lax.all_gather(piece, "seq", axis=0, tiled=True, axis_index_groups=same_core)
        sets, final = [], (None, gathered)
        arrived = piece

    facts = jnp.stack([after(kept_entry, arrived), row_owner, jnp.broadcast_to(kept_count, (slots,))])
    code_own, code_sib, code_column = pl.pallas_call(
        functools.partial(codes_kernel, positions, peers),
        out_shape=(
            jax.ShapeDtypeStruct((8, slots), jnp.float32),
            jax.ShapeDtypeStruct((8, slots), jnp.float32),
            jax.ShapeDtypeStruct((slots, 8), jnp.float32),
        ),
        in_specs=[VMEM, VMEM],
        out_specs=(VMEM, VMEM, VMEM),
        compiler_params=pltpu.CompilerParams(vmem_limit_bytes=8 * MIB),
        name="codes",
    )(facts, swap(facts, 1))

    first = [early_stats([block for _, block in some]) for some in sets]
    if stepwise:
        off, block = final
        sets.append([final, (off ^ 1, swap(after(block, beside[2], code_own), 2))])
    else:
        sets.append([final])
    blocks = [block for some in sets for _, block in some]
    offsets = [off for some in sets for off, _ in some]
    late = [block for _, block in sets[-1]]
    count = len(offsets)
    per_block = GROUP * blocks[0].shape[0]
    sent = pl.pallas_call(
        functools.partial(stats_kernel, offsets, [x.shape[0] for x in first], chips),
        out_shape=jax.ShapeDtypeStruct((chips, count, HALF, per_block), jnp.float32),
        in_specs=[SMEM] + [VMEM] * (2 + len(first) + len(late)),
        out_specs=VMEM,
        scratch_shapes=[pltpu.VMEM((count, HALF, per_block), jnp.float32)],
        compiler_params=pltpu.CompilerParams(vmem_limit_bytes=8 * MIB),
        cost_estimate=score_cost(late),
        name="late_stats",
    )(place, k_own, k_sib, *first, *late)

    score_row = -(-capacity // 8) * 8
    room = -(-(score_row + 8) // 16) * 16
    packed = pl.pallas_call(
        compact_kernel,
        out_shape=jax.ShapeDtypeStruct((peers, room, 2 * HEAD_DIM), jnp.bfloat16),
        in_specs=[VMEM, ANYWHERE, ANYWHERE],
        out_specs=VMEM,
        scratch_shapes=[
            pltpu.VMEM(cached_keys.shape, jnp.bfloat16),
            pltpu.VMEM(cached_values.shape, jnp.bfloat16),
            pltpu.VMEM((slots, 2 * HEAD_DIM), jnp.float32),
            pltpu.SemaphoreType.DMA((2,)),
        ],
        compiler_params=pltpu.CompilerParams(vmem_limit_bytes=GRANT),
        cost_estimate=pl.CostEstimate(
            flops=4 * slots * positions * KV_HEADS * HEAD_DIM,
            bytes_accessed=4 * positions * KV_HEADS * HEAD_DIM,
            transcendentals=0,
        ),
        name="compact",
    )(after(code_column, sent), cached_keys, cached_values)
    stats = lax.all_to_all(
        sent,
        "seq",
        split_axis=0,
        concat_axis=0,
        tiled=True,
        axis_index_groups=[[i for i in range(peers) if i % 2 == c] for c in range(2)],
    )
    factor = peers * positions / (GROUP * WINDOW * POOL)
    imp_own, imp_sib, sending = pl.pallas_call(
        functools.partial(mass_kernel, offsets, peers, factor, half_queries, len(edges), score_row),
        out_shape=(
            jax.ShapeDtypeStruct((HALF, positions), jnp.float32),
            jax.ShapeDtypeStruct((HALF, positions), jnp.float32),
            jax.ShapeDtypeStruct(packed.shape, packed.dtype),
        ),
        in_specs=[SMEM] + [VMEM] * 5 + [ANYWHERE] + [VMEM] * (len(edges) + count),
        out_specs=(VMEM, VMEM, VMEM),
        scratch_shapes=[
            pltpu.VMEM((count, HALF, per_block), jnp.float32),
            pltpu.VMEM((count * per_block, HEAD_DIM), jnp.float32),
            pltpu.SemaphoreType.DMA,
        ],
        compiler_params=pltpu.CompilerParams(vmem_limit_bytes=12 * MIB),
        cost_estimate=score_cost(blocks),
        name="mass",
    )(place, stats, k_own, k_sib, code_own, code_sib, packed, *edges, *blocks)

    got = lax.all_to_all(sending, "seq", split_axis=0, concat_axis=0, tiled=True)
    by_core = got[:, score_row : score_row + 2, :capacity].reshape(chips, 2, 2, capacity)
    score_out = by_core[:, 0] + by_core[:, 1]
    got_rows = got[:, :capacity]
    imp_other = swap(imp_sib, 1)
    importance = jnp.where(
        core == 0,
        jnp.concatenate([imp_own, imp_other], axis=0),
        jnp.concatenate([imp_other, imp_own], axis=0),
    )
    return (
        importance,
        got_rows.reshape(slots, 2 * HEAD_DIM),
        score_out.reshape(peers * capacity),
    )


def solution(mesh):
    in_specs = (
        P(("rep", "seq"), None),
        P(("rep", "seq"), None),
        P(("rep", "seq"), None),
        P(("rep", "seq")),
        P(("rep", "seq")),
        P(("rep", "seq")),
    )
    out_specs = (P("rep", "seq"), P(("rep", "seq"), None), P(("rep", "seq")))
    return jax.shard_map(
        per_device, mesh=mesh, in_specs=in_specs, out_specs=out_specs, check_vma=False
    )
```

```python
import functools

import jax
import jax.numpy as jnp
from jax import lax
from jax.experimental import pallas as pl
from jax.experimental.pallas import tpu as pltpu
from jax.sharding import PartitionSpec as P

HEADS = 64
KV_HEADS = 8
HEAD_DIM = 128
GROUP = 8
WINDOW = 128
POOL = 7
HALF = KV_HEADS // 2
EDGE = 16
SCALE2 = HEAD_DIM ** (-0.5) * 1.4426950408889634
MIB = 1 << 20

VMEM = pl.BlockSpec(memory_space=pltpu.VMEM)
SMEM = pl.BlockSpec(memory_space=pltpu.SMEM)
ANYWHERE = pl.BlockSpec(memory_space=pl.ANY)
GRANT = 56 * MIB


def nt(a, b, precision=None):
    return lax.dot_general(
        a, b, (((1,), (1,)), ((), ())), precision=precision, preferred_element_type=jnp.float32
    )


def one_hot(mask):
    return jnp.where(mask, 1.0, 0.0).astype(jnp.bfloat16)


def iota(shape, dim):
    return lax.broadcasted_iota(jnp.int32, shape, dim)


def codes_kernel(positions, peers, own_ref, sib_ref, own_code_ref, sib_code_ref, column_ref):
    for mine, ref, code_ref in ((True, own_ref, own_code_ref), (False, sib_ref, sib_code_ref)):
        slots = ref.shape[1]
        entry, owner, count = ref[0:1], ref[1:2], ref[2:3]
        capacity = slots // peers
        live = iota((1, slots), 1) < count
        member = jnp.where((owner == iota((peers, slots), 0)) & live, 1.0, 0.0)
        before = one_hot(iota((slots, slots), 0) < iota((slots, slots), 1))
        earlier = jnp.dot(member.astype(jnp.bfloat16), before, preferred_element_type=jnp.float32)
        rank = jnp.sum(earlier * member, axis=0, keepdims=True).astype(jnp.int32)
        target = jnp.where(live, owner * capacity + rank, -1)
        placed = one_hot(iota((slots, slots), 0) == target)
        token, head = entry % positions, entry // positions
        line = iota((8, slots), 0)
        facts = jnp.where(
            line == 0, 1, jnp.where(line == 1, head, jnp.where(line == 2, token // 64, token % 64))
        )
        facts = facts.astype(jnp.float32).astype(jnp.bfloat16)
        by_row = nt(facts, placed)
        row_token = jnp.where(by_row[0:1] > 0.5, by_row[2:3] * 64 + by_row[3:4], -1.0)
        code_ref[...] = jnp.where(line == 0, row_token, by_row[1:2])
        if mine:
            by_col = nt(placed, facts)
            col_token = jnp.where(by_col[:, 0:1] > 0.5, by_col[:, 2:3] * 64 + by_col[:, 3:4], -1.0)
            column = jnp.where(iota((slots, 8), 1) == 0, col_token, by_col[:, 1:2])
            column_ref[...] = column


def compact_kernel(column_ref, k_source, v_source, packed_ref, k_ref, v_ref, rows_ref, sems):
    copies = (
        pltpu.make_async_copy(k_source, k_ref, sems.at[0]),
        pltpu.make_async_copy(v_source, v_ref, sems.at[1]),
    )
    for copy in copies:
        copy.start()
    positions = k_ref.shape[0]
    slots = rows_ref.shape[0]
    token = column_ref[:, 0:1].astype(jnp.int32)
    head = column_ref[:, 1:2].astype(jnp.int32)
    pick = one_hot(iota((slots, positions), 1) == token)
    for side, source in enumerate((k_ref, v_ref)):
        copies[side].wait()
        kept = jnp.zeros((slots, HEAD_DIM), jnp.float32)
        for g in range(0, KV_HEADS, 2):
            pair = source[:, g * HEAD_DIM : (g + 2) * HEAD_DIM]
            found = jnp.dot(pick, pair, preferred_element_type=jnp.float32)
            kept = kept + jnp.where(head == g, found[:, :HEAD_DIM], 0.0)
            kept = kept + jnp.where(head == g + 1, found[:, HEAD_DIM:], 0.0)
        rows_ref[:, side * HEAD_DIM : (side + 1) * HEAD_DIM] = kept
    peers, room, width = packed_ref.shape
    capacity = slots // peers
    rest = jnp.zeros((room - 2 * capacity, width), jnp.float32)
    for p in range(peers):
        rows = rows_ref[p * capacity : (p + 1) * capacity, :]
        packed_ref[p] = jnp.concatenate([rows[:, :width], rows[:, width:], rest], axis=0).astype(
            jnp.bfloat16
        )


def query_rows(block_refs, g):
    parts = []
    for ref in block_refs:
        for h in range(GROUP):
            first = (g * GROUP + h) * HEAD_DIM
            parts.append(ref[:, first : first + HEAD_DIM])
    return jnp.concatenate(parts, axis=0)


def spread(limits, value):
    low, high = limits
    return jnp.minimum(low, jnp.min(value)), jnp.maximum(high, jnp.max(value))


def local_stats(block_refs, k_refs, store):
    per_block = GROUP * block_refs[0].shape[0]
    tokens = k_refs[0].shape[0]

    def keep(g, lse):
        for b in range(len(block_refs)):
            store(b, g, lse[:, b * per_block : (b + 1) * per_block])

    limits = (jnp.float32(jnp.inf), jnp.float32(-jnp.inf))
    step = min(512, tokens)
    for g in range(HALF):
        rows = query_rows(block_refs, g)
        count = rows.shape[0]
        total = jnp.zeros((8, count), jnp.float32)
        cols = slice(g * HEAD_DIM, (g + 1) * HEAD_DIM)
        for k_ref in k_refs:
            for start in range(0, tokens, step):
                weights = jnp.exp2(nt(k_ref[start : start + step, cols], rows) * SCALE2)
                total = total + jnp.sum(weights.reshape(step // 8, 8, count), axis=0)
        total = jnp.sum(total, axis=0, keepdims=True)
        limits = spread(limits, total)
        keep(g, jnp.log2(total))

    in_range = (limits[0] > 2.0**-60) & (limits[1] < 2.0**100)

    @pl.when(jnp.logical_not(in_range))
    def _():
        part = min(256, tokens)
        for g in range(HALF):
            rows = query_rows(block_refs, g)
            count = rows.shape[0]
            carry = (jnp.full((1, count), -jnp.inf, jnp.float32), jnp.zeros((1, count), jnp.float32))
            cols = slice(g * HEAD_DIM, (g + 1) * HEAD_DIM)
            for k_ref in k_refs:

                def advance(j, carry):
                    peak, total = carry
                    start = pl.multiple_of(j * part, part)
                    scores = nt(k_ref[pl.ds(start, part), cols], rows)
                    higher = jnp.maximum(peak, jnp.max(scores, axis=0, keepdims=True))
                    total = total * jnp.exp2((peak - higher) * SCALE2) + jnp.sum(
                        jnp.exp2((scores - higher) * SCALE2), axis=0, keepdims=True
                    )
                    return higher, total

                carry = lax.fori_loop(0, tokens // part, advance, carry)
            keep(g, carry[0] * SCALE2 + jnp.log2(carry[1]))


def sender(chip, offset):
    return 0 if offset is None else chip ^ offset


def early_stats_kernel(count, *refs):
    blocks, k_refs, out_ref = refs[:count], refs[count : count + 2], refs[-1]

    def store(b, g, lse):
        out_ref[b, g : g + 1, :] = lse

    local_stats(blocks, k_refs, store)


def stats_kernel(offsets, early, dests, *refs):
    place_ref, k_refs = refs[0], refs[1:3]
    out_ref, hold = refs[-2:]
    chip = place_ref[0] // 2
    done = 0
    for ref, size in zip(refs[3:], early):
        for b in range(size):
            hold[sender(chip, offsets[done + b])] = ref[b]
        done += size

    def store(b, g, lse):
        hold[sender(chip, offsets[done + b]), g : g + 1, :] = lse

    local_stats(refs[3 + len(early) : -2], k_refs, store)
    everything = hold[...]
    for d in range(dests):
        out_ref[d] = everything


def split3(x):
    high = x.astype(jnp.bfloat16)
    rest = x - high.astype(jnp.float32)
    middle = rest.astype(jnp.bfloat16)
    low = (rest - middle.astype(jnp.float32)).astype(jnp.bfloat16)
    return high, middle, low


def mass_kernel(offsets, peers, factor, width, edges, score_row, *refs):
    count = len(offsets)
    place_ref, stats_ref, k_own, k_sib = refs[:4]
    codes, packed_ref = refs[4:6], refs[6]
    edge_refs, refs = refs[7 : 7 + edges], refs[7 + edges :]
    blocks = refs[:count]
    imp_own, imp_sib, out_ref, lse_ref, side_ref = refs[count:]
    tokens = k_own.shape[0]
    core = place_ref[0] % 2
    chip = place_ref[0] // 2
    chips = peers // 2
    is_low = core == 0

    stats = stats_ref[...]
    top = jnp.max(stats, axis=0)
    lse_ref[...] = top + jnp.log2(jnp.sum(jnp.exp2(stats - top[None]), axis=0))

    step = min(512, tokens)
    found = [[], []]
    rims = []
    for g in range(HALF):
        rows = query_rows(blocks, g)
        lse = jnp.concatenate([lse_ref[sender(chip, off), g : g + 1, :] for off in offsets], axis=1)
        parts = jnp.concatenate(
            split3(lse) + (jnp.zeros((5, lse.shape[1]), jnp.bfloat16),), axis=0
        )
        side_ref[...] = lax.dot_general(
            parts, jnp.ones((8, HEAD_DIM), jnp.bfloat16), (((0,), (0,)), ((), ())),
            preferred_element_type=jnp.float32,
        )
        cols = slice(g * HEAD_DIM, (g + 1) * HEAD_DIM)
        for i, k_ref in enumerate((k_own, k_sib)):
            line = []
            for start in range(0, tokens, step):
                shift = jnp.concatenate([side_ref[...]] * (step // HEAD_DIM), axis=1)
                weights = jnp.exp2(nt(rows, k_ref[start : start + step, cols]) * SCALE2 - shift)
                line.append(jnp.sum(weights, axis=0, keepdims=True))
            found[i].append(jnp.concatenate(line, axis=1))
        if edges:
            low = slice(g * HEAD_DIM, (g + 1) * HEAD_DIM)
            high = slice((HALF + g) * HEAD_DIM, (HALF + g + 1) * HEAD_DIM)
            rim_keys = [jnp.where(is_low, ref[:, low], ref[:, high]) for ref in edge_refs]
        else:
            cols = slice(width + g * HEAD_DIM, width + (g + 1) * HEAD_DIM)
            rim_keys = []
            for other in (chip ^ jnp.maximum(chip - 1, 0), chip ^ jnp.minimum(chip + 1, chips - 1)):
                found_keys = blocks[0][:, cols]
                for off, ref in zip(offsets[1:], blocks[1:]):
                    found_keys = jnp.where(other == off, ref[:, cols], found_keys)
                rim_keys.append(found_keys)
        weights = jnp.exp2(nt(jnp.concatenate(rim_keys, axis=0), rows) * SCALE2 - lse)
        folded = weights[:, 0:HEAD_DIM]
        for first in range(HEAD_DIM, weights.shape[1], HEAD_DIM):
            folded = folded + weights[:, first : first + HEAD_DIM]
        rims.append(jnp.sum(folded.T, axis=0, keepdims=True))
    own = jnp.concatenate(found[0], axis=0)
    sib = jnp.concatenate(found[1], axis=0)
    rim = jnp.concatenate(rims, axis=0)
    first = jnp.where(is_low, own, sib)
    second = jnp.where(is_low, sib, own)
    side = POOL // 2
    if edges:
        rim_own, rim_sib = rim[:, :EDGE], rim[:, EDGE : 2 * EDGE]
        before = jnp.where(is_low, rim_own, rim_sib)[:, EDGE - side :]
        after = jnp.where(is_low, rim_sib, rim_own)[:, :side]
    else:
        size = blocks[0].shape[0]
        mid = size // 2
        before = jnp.where(is_low, rim[:, size - side : size], rim[:, mid - side : mid])
        after = jnp.where(is_low, rim[:, size : size + side], rim[:, size + mid : size + mid + side])
    before = jnp.where(chip == 0, 0.0, before)
    after = jnp.where(chip == chips - 1, 0.0, after)
    padded = jnp.concatenate([before, first, second, after], axis=1)
    pooled = padded[:, 0 : 2 * tokens]
    for shift in range(1, POOL):
        pooled = pooled + padded[:, shift : shift + 2 * tokens]
    importance = pooled * factor
    halves = (importance[:, :tokens], importance[:, tokens:])
    imp_own[...] = jnp.where(is_low, halves[0], halves[1])
    imp_sib[...] = jnp.where(is_low, halves[1], halves[0])
    slots = codes[0].shape[1]
    capacity = slots // peers
    scores = []
    for side in range(2):
        code = jnp.where(core == side, codes[0][...], codes[1][...]).astype(jnp.int32)
        parts = jnp.concatenate(split3(halves[side]), axis=0)
        pick = one_hot(iota((tokens, slots), 0) == code[0:1])
        hits = jnp.dot(parts, pick, preferred_element_type=jnp.float32)
        value = hits[0:HALF] + hits[HALF : 2 * HALF] + hits[2 * HALF : 3 * HALF]
        mine = iota((HALF, slots), 0) + core * HALF == code[1:2]
        scores.append(jnp.sum(jnp.where(mine, value, 0.0), axis=0, keepdims=True))
    both = jnp.concatenate(scores + [jnp.zeros((6, slots), jnp.float32)], axis=0)
    for p in range(peers):
        some = both[:, p * capacity : (p + 1) * capacity]
        some = jnp.concatenate([some, jnp.zeros((8, HEAD_DIM - capacity), jnp.float32)], axis=1)
        out_ref[p] = jnp.concatenate(
            [packed_ref[p, 0:score_row, :], some.astype(jnp.bfloat16)], axis=0
        )


def after(x, *earlier):
    return lax.optimization_barrier((x, earlier))[0]


def per_device(cached_keys, cached_values, window_queries, kept_count, kept_entry, row_owner):
    positions = cached_keys.shape[0]
    peers = lax.axis_size("seq")
    chips = peers // 2
    slots = kept_entry.shape[0]
    capacity = slots // peers
    me = lax.axis_index("seq")
    core = me % 2
    place = me.astype(jnp.int32).reshape(1)
    half_keys = HALF * HEAD_DIM
    half_queries = HALF * GROUP * HEAD_DIM

    def swap(x, distance):
        return lax.ppermute(x, "seq", [(i, i ^ distance) for i in range(peers)])

    def half(x, which, width):
        return lax.dynamic_slice_in_dim(x, which * width, width, axis=1)

    def joined(parts):
        return jnp.concatenate(parts, axis=0)

    sibling_queries = swap(window_queries, 1)
    own_queries = half(window_queries, core, half_queries)
    ready_keys = after(cached_keys, sibling_queries)
    k_other = half(ready_keys, 1 - core, half_keys)
    k_sib = swap(k_other, 1)

    lines = chips // 2
    shard_rows = window_queries.shape[0]
    stepwise = shard_rows % 8 == 0 and chips % 4 == 0 and lines & (lines - 1) == 0
    edge = shard_rows if stepwise else EDGE
    rim = jnp.where(core == 1, cached_keys[positions - edge :], cached_keys[:edge])
    pair = [own_queries, half(sibling_queries, core, half_queries)]
    if stepwise:
        sibling_rim = swap(rim, 1)
        ends = [half(rim, core, half_keys), half(sibling_rim, core, half_keys)]
        piece = joined([jnp.concatenate(x, axis=1) for x in zip(pair, ends)])
        edges = []
    else:
        piece = joined(pair)
        offsets = [None]
        ring = [(2 * i + 1, 2 * i + 2) for i in range(chips - 1)]
        edge_own = lax.ppermute(rim, "seq", ring + [(b, a) for a, b in ring])
        edges = [edge_own, swap(edge_own, 1)]

    def score_cost(some):
        queries = len(some) * HALF * GROUP * some[0].shape[0]
        return pl.CostEstimate(
            flops=4 * queries * positions * HEAD_DIM,
            bytes_accessed=2 * positions * half_keys,
            transcendentals=0,
        )

    def early_stats(some):
        shape = (len(some), HALF, GROUP * some[0].shape[0])
        return pl.pallas_call(
            functools.partial(early_stats_kernel, len(some)),
            out_shape=jax.ShapeDtypeStruct(shape, jnp.float32),
            in_specs=[VMEM] * (len(some) + 2),
            out_specs=VMEM,
            compiler_params=pltpu.CompilerParams(vmem_limit_bytes=8 * MIB),
            cost_estimate=score_cost(some),
            name="early_stats",
        )(*some, k_own, k_sib)

    if stepwise:
        line, distance = [(0, piece)], lines // 2
        beside = {0: swap(piece, 2)}
        while distance:
            for off, block in list(line):
                if distance == 1 and off == 0:
                    near = swap(block, 4)
                    line.append((2, near))
                else:
                    if distance == 1:
                        block = after(block, near, beside[0])
                    line.append((off ^ 2 * distance, swap(block, 4 * distance)))
            distance //= 2
        beside.update({off: swap(block, 2) for off, block in line[1:-1]})
        start = [(0, piece), (1, beside[0]), (2, near), (3, beside[2])]
        sets = [start]
        for off, block in line[:-1]:
            if off not in (0, 2):
                sets.append([(off, block), (off ^ 1, beside[off])])
        final = line[-1]
        arrived = (line[1][1], near, beside[0])
    else:
        same_core = [[i for i in range(peers) if i % 2 == c] for c in range(2)]
        gathered = lax.all_gather(piece, "seq", axis=0, tiled=True, axis_index_groups=same_core)
        sets, final = [], (None, gathered)
        arrived = piece

    facts = jnp.stack([after(kept_entry, arrived), row_owner, jnp.broadcast_to(kept_count, (slots,))])
    code_own, code_sib, code_column = pl.pallas_call(
        functools.partial(codes_kernel, positions, peers),
        out_shape=(
            jax.ShapeDtypeStruct((8, slots), jnp.float32),
            jax.ShapeDtypeStruct((8, slots), jnp.float32),
            jax.ShapeDtypeStruct((slots, 8), jnp.float32),
        ),
        in_specs=[VMEM, VMEM],
        out_specs=(VMEM, VMEM, VMEM),
        compiler_params=pltpu.CompilerParams(vmem_limit_bytes=8 * MIB),
        name="codes",
    )(facts, swap(facts, 1))

    k_own = half(after(cached_keys, arrived), core, half_keys)
    first = []
    for some in sets:
        here = [block for _, block in some]
        if first:
            here[0] = after(here[0], first[-1])
        first.append(early_stats(here))
    if stepwise:
        off, block = final
        sets.append([final, (off ^ 1, swap(after(block, beside[2], code_own), 2))])
    else:
        sets.append([final])
    blocks = [block for some in sets for _, block in some]
    offsets = [off for some in sets for off, _ in some]
    late = [block for _, block in sets[-1]]
    count = len(offsets)
    per_block = GROUP * blocks[0].shape[0]
    sent = pl.pallas_call(
        functools.partial(stats_kernel, offsets, [x.shape[0] for x in first], chips),
        out_shape=jax.ShapeDtypeStruct((chips, count, HALF, per_block), jnp.float32),
        in_specs=[SMEM] + [VMEM] * (2 + len(first) + len(late)),
        out_specs=VMEM,
        scratch_shapes=[pltpu.VMEM((count, HALF, per_block), jnp.float32)],
        compiler_params=pltpu.CompilerParams(vmem_limit_bytes=8 * MIB),
        cost_estimate=score_cost(late),
        name="late_stats",
    )(place, k_own, k_sib, *first, *late)

    score_row = -(-2 * capacity // 16) * 16
    room = score_row + 8
    packed = pl.pallas_call(
        compact_kernel,
        out_shape=jax.ShapeDtypeStruct((peers, room, HEAD_DIM), jnp.bfloat16),
        in_specs=[VMEM, ANYWHERE, ANYWHERE],
        out_specs=VMEM,
        scratch_shapes=[
            pltpu.VMEM(cached_keys.shape, jnp.bfloat16),
            pltpu.VMEM(cached_values.shape, jnp.bfloat16),
            pltpu.VMEM((slots, 2 * HEAD_DIM), jnp.float32),
            pltpu.SemaphoreType.DMA((2,)),
        ],
        compiler_params=pltpu.CompilerParams(vmem_limit_bytes=GRANT),
        cost_estimate=pl.CostEstimate(
            flops=4 * slots * positions * KV_HEADS * HEAD_DIM,
            bytes_accessed=4 * positions * KV_HEADS * HEAD_DIM,
            transcendentals=0,
        ),
        name="compact",
    )(after(code_column, sent), cached_keys, cached_values)
    stats = lax.all_to_all(
        sent,
        "seq",
        split_axis=0,
        concat_axis=0,
        tiled=True,
        axis_index_groups=[[i for i in range(peers) if i % 2 == c] for c in range(2)],
    )
    factor = peers * positions / (GROUP * WINDOW * POOL)
    imp_own, imp_sib, sending = pl.pallas_call(
        functools.partial(mass_kernel, offsets, peers, factor, half_queries, len(edges), score_row),
        out_shape=(
            jax.ShapeDtypeStruct((HALF, positions), jnp.float32),
            jax.ShapeDtypeStruct((HALF, positions), jnp.float32),
            jax.ShapeDtypeStruct(packed.shape, packed.dtype),
        ),
        in_specs=[SMEM] + [VMEM] * (6 + len(edges) + count),
        out_specs=(VMEM, VMEM, VMEM),
        scratch_shapes=[
            pltpu.VMEM((count, HALF, per_block), jnp.float32),
            pltpu.VMEM((count * per_block, HEAD_DIM), jnp.float32),
        ],
        compiler_params=pltpu.CompilerParams(vmem_limit_bytes=12 * MIB),
        cost_estimate=score_cost(blocks),
        name="mass",
    )(place, stats, k_own, k_sib, code_own, code_sib, packed, *edges, *blocks)

    got = lax.all_to_all(sending, "seq", split_axis=0, concat_axis=0, tiled=True)
    by_core = got[:, score_row : score_row + 2, :capacity].reshape(chips, 2, 2, capacity)
    score_out = by_core[:, 0] + by_core[:, 1]
    got_rows = jnp.concatenate([got[:, :capacity], got[:, capacity : 2 * capacity]], axis=2)
    imp_other = swap(imp_sib, 1)
    importance = jnp.where(
        core == 0,
        jnp.concatenate([imp_own, imp_other], axis=0),
        jnp.concatenate([imp_other, imp_own], axis=0),
    )
    return (
        importance,
        got_rows.reshape(slots, 2 * HEAD_DIM),
        score_out.reshape(peers * capacity),
    )


def solution(mesh):
    in_specs = (
        P(("rep", "seq"), None),
        P(("rep", "seq"), None),
        P(("rep", "seq"), None),
        P(("rep", "seq")),
        P(("rep", "seq")),
        P(("rep", "seq")),
    )
    out_specs = (P("rep", "seq"), P(("rep", "seq"), None), P(("rep", "seq")))
    return jax.shard_map(
        per_device, mesh=mesh, in_specs=in_specs, out_specs=out_specs, check_vma=False
    )
```

```python
import functools

import jax
import jax.numpy as jnp
from jax import lax
from jax.experimental import pallas as pl
from jax.experimental.pallas import tpu as pltpu
from jax.sharding import PartitionSpec as P

HEADS = 64
KV_HEADS = 8
HEAD_DIM = 128
GROUP = 8
WINDOW = 128
POOL = 7
HALF = KV_HEADS // 2
EDGE = 16
SCALE2 = HEAD_DIM ** (-0.5) * 1.4426950408889634
MIB = 1 << 20

VMEM = pl.BlockSpec(memory_space=pltpu.VMEM)
SMEM = pl.BlockSpec(memory_space=pltpu.SMEM)
ANYWHERE = pl.BlockSpec(memory_space=pl.ANY)
GRANT = 56 * MIB


def nt(a, b, precision=None):
    return lax.dot_general(
        a, b, (((1,), (1,)), ((), ())), precision=precision, preferred_element_type=jnp.float32
    )


def one_hot(mask):
    return jnp.where(mask, 1.0, 0.0).astype(jnp.bfloat16)


def iota(shape, dim):
    return lax.broadcasted_iota(jnp.int32, shape, dim)


def codes_kernel(positions, peers, own_ref, sib_ref, own_code_ref, sib_code_ref, column_ref):
    for mine, ref, code_ref in ((True, own_ref, own_code_ref), (False, sib_ref, sib_code_ref)):
        slots = ref.shape[1]
        entry, owner, count = ref[0:1], ref[1:2], ref[2:3]
        capacity = slots // peers
        live = iota((1, slots), 1) < count
        member = jnp.where((owner == iota((peers, slots), 0)) & live, 1.0, 0.0)
        before = one_hot(iota((slots, slots), 0) < iota((slots, slots), 1))
        earlier = jnp.dot(member.astype(jnp.bfloat16), before, preferred_element_type=jnp.float32)
        rank = jnp.sum(earlier * member, axis=0, keepdims=True).astype(jnp.int32)
        target = jnp.where(live, owner * capacity + rank, -1)
        placed = one_hot(iota((slots, slots), 0) == target)
        token, head = entry % positions, entry // positions
        line = iota((8, slots), 0)
        facts = jnp.where(
            line == 0, 1, jnp.where(line == 1, head, jnp.where(line == 2, token // 64, token % 64))
        )
        facts = facts.astype(jnp.float32).astype(jnp.bfloat16)
        by_row = nt(facts, placed)
        row_token = jnp.where(by_row[0:1] > 0.5, by_row[2:3] * 64 + by_row[3:4], -1.0)
        code_ref[...] = jnp.where(line == 0, row_token, by_row[1:2])
        if mine:
            by_col = nt(placed, facts)
            col_token = jnp.where(by_col[:, 0:1] > 0.5, by_col[:, 2:3] * 64 + by_col[:, 3:4], -1.0)
            column = jnp.where(iota((slots, 8), 1) == 0, col_token, by_col[:, 1:2])
            column_ref[...] = column


def compact_kernel(
    place_ref, column_ref, k_own_ref, k_other_ref, v_source, packed_ref, v_ref, rows_ref, sem
):
    copy = pltpu.make_async_copy(v_source, v_ref, sem)
    copy.start()
    positions = v_ref.shape[0]
    slots = rows_ref.shape[0]
    core = place_ref[0] % 2
    token = column_ref[:, 0:1].astype(jnp.int32)
    head = column_ref[:, 1:2].astype(jnp.int32)
    pick = one_hot(iota((slots, positions), 1) == token)

    def kept(source, heads, first, so_far):
        for g in range(0, heads, 2):
            pair = source[:, g * HEAD_DIM : (g + 2) * HEAD_DIM]
            found = jnp.dot(pick, pair, preferred_element_type=jnp.float32)
            so_far = so_far + jnp.where(head == first + g, found[:, :HEAD_DIM], 0.0)
            so_far = so_far + jnp.where(head == first + g + 1, found[:, HEAD_DIM:], 0.0)
        return so_far

    none = jnp.zeros((slots, HEAD_DIM), jnp.float32)
    keys = kept(k_own_ref, HALF, core * HALF, none)
    rows_ref[:, :HEAD_DIM] = kept(k_other_ref, HALF, (1 - core) * HALF, keys)
    copy.wait()
    rows_ref[:, HEAD_DIM:] = kept(v_ref, KV_HEADS, 0, none)
    peers, room, width = packed_ref.shape
    capacity = slots // peers
    rest = jnp.zeros((room - 2 * capacity, width), jnp.float32)
    for p in range(peers):
        rows = rows_ref[p * capacity : (p + 1) * capacity, :]
        packed_ref[p] = jnp.concatenate([rows[:, :width], rows[:, width:], rest], axis=0).astype(
            jnp.bfloat16
        )


def query_rows(block_refs, g):
    parts = []
    for ref in block_refs:
        for h in range(GROUP):
            first = (g * GROUP + h) * HEAD_DIM
            parts.append(ref[:, first : first + HEAD_DIM])
    return jnp.concatenate(parts, axis=0)


def spread(limits, value):
    low, high = limits
    return jnp.minimum(low, jnp.min(value)), jnp.maximum(high, jnp.max(value))


def local_stats(block_refs, k_refs, store):
    per_block = GROUP * block_refs[0].shape[0]
    tokens = k_refs[0].shape[0]

    def keep(g, lse):
        for b in range(len(block_refs)):
            store(b, g, lse[:, b * per_block : (b + 1) * per_block])

    limits = (jnp.float32(jnp.inf), jnp.float32(-jnp.inf))
    step = min(512, tokens)
    for g in range(HALF):
        rows = query_rows(block_refs, g)
        count = rows.shape[0]
        total = jnp.zeros((8, count), jnp.float32)
        cols = slice(g * HEAD_DIM, (g + 1) * HEAD_DIM)
        for k_ref in k_refs:
            for start in range(0, tokens, step):
                weights = jnp.exp2(nt(k_ref[start : start + step, cols], rows) * SCALE2)
                total = total + jnp.sum(weights.reshape(step // 8, 8, count), axis=0)
        total = jnp.sum(total, axis=0, keepdims=True)
        limits = spread(limits, total)
        keep(g, jnp.log2(total))

    in_range = (limits[0] > 2.0**-60) & (limits[1] < 2.0**100)

    @pl.when(jnp.logical_not(in_range))
    def _():
        part = min(256, tokens)
        for g in range(HALF):
            rows = query_rows(block_refs, g)
            count = rows.shape[0]
            carry = (jnp.full((1, count), -jnp.inf, jnp.float32), jnp.zeros((1, count), jnp.float32))
            cols = slice(g * HEAD_DIM, (g + 1) * HEAD_DIM)
            for k_ref in k_refs:

                def advance(j, carry):
                    peak, total = carry
                    start = pl.multiple_of(j * part, part)
                    scores = nt(k_ref[pl.ds(start, part), cols], rows)
                    higher = jnp.maximum(peak, jnp.max(scores, axis=0, keepdims=True))
                    total = total * jnp.exp2((peak - higher) * SCALE2) + jnp.sum(
                        jnp.exp2((scores - higher) * SCALE2), axis=0, keepdims=True
                    )
                    return higher, total

                carry = lax.fori_loop(0, tokens // part, advance, carry)
            keep(g, carry[0] * SCALE2 + jnp.log2(carry[1]))


def sender(chip, offset):
    return 0 if offset is None else chip ^ offset


def early_stats_kernel(count, *refs):
    blocks, k_refs, out_ref = refs[:count], refs[count : count + 2], refs[-1]

    def store(b, g, lse):
        out_ref[b, g : g + 1, :] = lse

    local_stats(blocks, k_refs, store)


def stats_kernel(offsets, early, dests, *refs):
    place_ref, k_refs = refs[0], refs[1:3]
    out_ref, hold = refs[-2:]
    chip = place_ref[0] // 2
    done = 0
    for ref, size in zip(refs[3:], early):
        for b in range(size):
            hold[sender(chip, offsets[done + b])] = ref[b]
        done += size

    def store(b, g, lse):
        hold[sender(chip, offsets[done + b]), g : g + 1, :] = lse

    local_stats(refs[3 + len(early) : -2], k_refs, store)
    everything = hold[...]
    for d in range(dests):
        out_ref[d] = everything


def split3(x):
    high = x.astype(jnp.bfloat16)
    rest = x - high.astype(jnp.float32)
    middle = rest.astype(jnp.bfloat16)
    low = (rest - middle.astype(jnp.float32)).astype(jnp.bfloat16)
    return high, middle, low


def mass_kernel(offsets, peers, factor, width, edges, score_row, *refs):
    count = len(offsets)
    place_ref, stats_ref, k_own, k_sib = refs[:4]
    codes, packed_ref = refs[4:6], refs[6]
    edge_refs, refs = refs[7 : 7 + edges], refs[7 + edges :]
    blocks = refs[:count]
    imp_own, imp_sib, out_ref, lse_ref, side_ref = refs[count:]
    tokens = k_own.shape[0]
    core = place_ref[0] % 2
    chip = place_ref[0] // 2
    chips = peers // 2
    is_low = core == 0

    stats = stats_ref[...]
    top = jnp.max(stats, axis=0)
    lse_ref[...] = top + jnp.log2(jnp.sum(jnp.exp2(stats - top[None]), axis=0))

    step = min(512, tokens)
    found = [[], []]
    rims = []
    for g in range(HALF):
        rows = query_rows(blocks, g)
        lse = jnp.concatenate([lse_ref[sender(chip, off), g : g + 1, :] for off in offsets], axis=1)
        parts = jnp.concatenate(
            split3(lse) + (jnp.zeros((5, lse.shape[1]), jnp.bfloat16),), axis=0
        )
        side_ref[...] = lax.dot_general(
            parts, jnp.ones((8, HEAD_DIM), jnp.bfloat16), (((0,), (0,)), ((), ())),
            preferred_element_type=jnp.float32,
        )
        cols = slice(g * HEAD_DIM, (g + 1) * HEAD_DIM)
        for i, k_ref in enumerate((k_own, k_sib)):
            line = []
            for start in range(0, tokens, step):
                shift = jnp.concatenate([side_ref[...]] * (step // HEAD_DIM), axis=1)
                weights = jnp.exp2(nt(rows, k_ref[start : start + step, cols]) * SCALE2 - shift)
                line.append(jnp.sum(weights, axis=0, keepdims=True))
            found[i].append(jnp.concatenate(line, axis=1))
        if edges:
            low = slice(g * HEAD_DIM, (g + 1) * HEAD_DIM)
            high = slice((HALF + g) * HEAD_DIM, (HALF + g + 1) * HEAD_DIM)
            rim_keys = [jnp.where(is_low, ref[:, low], ref[:, high]) for ref in edge_refs]
        else:
            cols = slice(width + g * HEAD_DIM, width + (g + 1) * HEAD_DIM)
            rim_keys = []
            for other in (chip ^ jnp.maximum(chip - 1, 0), chip ^ jnp.minimum(chip + 1, chips - 1)):
                found_keys = blocks[0][:, cols]
                for off, ref in zip(offsets[1:], blocks[1:]):
                    found_keys = jnp.where(other == off, ref[:, cols], found_keys)
                rim_keys.append(found_keys)
        weights = jnp.exp2(nt(jnp.concatenate(rim_keys, axis=0), rows) * SCALE2 - lse)
        folded = weights[:, 0:HEAD_DIM]
        for first in range(HEAD_DIM, weights.shape[1], HEAD_DIM):
            folded = folded + weights[:, first : first + HEAD_DIM]
        rims.append(jnp.sum(folded.T, axis=0, keepdims=True))
    own = jnp.concatenate(found[0], axis=0)
    sib = jnp.concatenate(found[1], axis=0)
    rim = jnp.concatenate(rims, axis=0)
    first = jnp.where(is_low, own, sib)
    second = jnp.where(is_low, sib, own)
    side = POOL // 2
    if edges:
        rim_own, rim_sib = rim[:, :EDGE], rim[:, EDGE : 2 * EDGE]
        before = jnp.where(is_low, rim_own, rim_sib)[:, EDGE - side :]
        after = jnp.where(is_low, rim_sib, rim_own)[:, :side]
    else:
        size = blocks[0].shape[0]
        mid = size // 2
        before = jnp.where(is_low, rim[:, size - side : size], rim[:, mid - side : mid])
        after = jnp.where(is_low, rim[:, size : size + side], rim[:, size + mid : size + mid + side])
    before = jnp.where(chip == 0, 0.0, before)
    after = jnp.where(chip == chips - 1, 0.0, after)
    padded = jnp.concatenate([before, first, second, after], axis=1)
    pooled = padded[:, 0 : 2 * tokens]
    for shift in range(1, POOL):
        pooled = pooled + padded[:, shift : shift + 2 * tokens]
    importance = pooled * factor
    halves = (importance[:, :tokens], importance[:, tokens:])
    imp_own[...] = jnp.where(is_low, halves[0], halves[1])
    imp_sib[...] = jnp.where(is_low, halves[1], halves[0])
    slots = codes[0].shape[1]
    capacity = slots // peers
    scores = []
    for side in range(2):
        code = jnp.where(core == side, codes[0][...], codes[1][...]).astype(jnp.int32)
        parts = jnp.concatenate(split3(halves[side]), axis=0)
        pick = one_hot(iota((tokens, slots), 0) == code[0:1])
        hits = jnp.dot(parts, pick, preferred_element_type=jnp.float32)
        value = hits[0:HALF] + hits[HALF : 2 * HALF] + hits[2 * HALF : 3 * HALF]
        mine = iota((HALF, slots), 0) + core * HALF == code[1:2]
        scores.append(jnp.sum(jnp.where(mine, value, 0.0), axis=0, keepdims=True))
    both = jnp.concatenate(scores + [jnp.zeros((6, slots), jnp.float32)], axis=0)
    for p in range(peers):
        some = both[:, p * capacity : (p + 1) * capacity]
        some = jnp.concatenate([some, jnp.zeros((8, HEAD_DIM - capacity), jnp.float32)], axis=1)
        out_ref[p] = jnp.concatenate(
            [packed_ref[p, 0:score_row, :], some.astype(jnp.bfloat16)], axis=0
        )


def after(x, *earlier):
    return lax.optimization_barrier((x, earlier))[0]


def per_device(cached_keys, cached_values, window_queries, kept_count, kept_entry, row_owner):
    positions = cached_keys.shape[0]
    peers = lax.axis_size("seq")
    chips = peers // 2
    slots = kept_entry.shape[0]
    capacity = slots // peers
    me = lax.axis_index("seq")
    core = me % 2
    place = me.astype(jnp.int32).reshape(1)
    half_keys = HALF * HEAD_DIM
    half_queries = HALF * GROUP * HEAD_DIM

    def swap(x, distance):
        return lax.ppermute(x, "seq", [(i, i ^ distance) for i in range(peers)])

    def half(x, which, width):
        return lax.dynamic_slice_in_dim(x, which * width, width, axis=1)

    def joined(parts):
        return jnp.concatenate(parts, axis=0)

    sibling_queries = swap(window_queries, 1)
    own_queries = half(window_queries, core, half_queries)
    ready_keys = after(cached_keys, sibling_queries)
    k_other = half(ready_keys, 1 - core, half_keys)
    k_sib = swap(k_other, 1)

    lines = chips // 2
    shard_rows = window_queries.shape[0]
    stepwise = shard_rows % 8 == 0 and chips % 4 == 0 and lines & (lines - 1) == 0
    edge = shard_rows if stepwise else EDGE
    rim = jnp.where(core == 1, cached_keys[positions - edge :], cached_keys[:edge])
    pair = [own_queries, half(sibling_queries, core, half_queries)]
    if stepwise:
        sibling_rim = swap(rim, 1)
        ends = [half(rim, core, half_keys), half(sibling_rim, core, half_keys)]
        piece = joined([jnp.concatenate(x, axis=1) for x in zip(pair, ends)])
        edges = []
    else:
        piece = joined(pair)
        offsets = [None]
        ring = [(2 * i + 1, 2 * i + 2) for i in range(chips - 1)]
        edge_own = lax.ppermute(rim, "seq", ring + [(b, a) for a, b in ring])
        edges = [edge_own, swap(edge_own, 1)]

    def score_cost(some):
        queries = len(some) * HALF * GROUP * some[0].shape[0]
        return pl.CostEstimate(
            flops=4 * queries * positions * HEAD_DIM,
            bytes_accessed=2 * positions * half_keys,
            transcendentals=0,
        )

    def early_stats(some):
        shape = (len(some), HALF, GROUP * some[0].shape[0])
        return pl.pallas_call(
            functools.partial(early_stats_kernel, len(some)),
            out_shape=jax.ShapeDtypeStruct(shape, jnp.float32),
            in_specs=[VMEM] * (len(some) + 2),
            out_specs=VMEM,
            compiler_params=pltpu.CompilerParams(vmem_limit_bytes=8 * MIB),
            cost_estimate=score_cost(some),
            name="early_stats",
        )(*some, k_own, k_sib)

    if stepwise:
        line, distance = [(0, piece)], lines // 2
        beside = {0: swap(piece, 2)}
        while distance:
            for off, block in list(line):
                if distance == 1 and off == 0:
                    near = swap(block, 4)
                    line.append((2, near))
                else:
                    if distance == 1:
                        block = after(block, beside[0], near)
                    line.append((off ^ 2 * distance, swap(block, 4 * distance)))
            distance //= 2
        beside.update({off: swap(block, 2) for off, block in line[1:-1]})
        start = [(0, piece), (1, beside[0]), (2, near), (3, beside[2])]
        sets = [start]
        for off, block in line[:-1]:
            if off not in (0, 2):
                sets.append([(off, block), (off ^ 1, beside[off])])
        final = line[-1]
        arrived = (beside[0], near, line[1][1])
    else:
        same_core = [[i for i in range(peers) if i % 2 == c] for c in range(2)]
        gathered = lax.all_gather(piece, "seq", axis=0, tiled=True, axis_index_groups=same_core)
        sets, final = [], (None, gathered)
        arrived = piece

    facts = jnp.stack([after(kept_entry, arrived), row_owner, jnp.broadcast_to(kept_count, (slots,))])
    code_own, code_sib, code_column = pl.pallas_call(
        functools.partial(codes_kernel, positions, peers),
        out_shape=(
            jax.ShapeDtypeStruct((8, slots), jnp.float32),
            jax.ShapeDtypeStruct((8, slots), jnp.float32),
            jax.ShapeDtypeStruct((slots, 8), jnp.float32),
        ),
        in_specs=[VMEM, VMEM],
        out_specs=(VMEM, VMEM, VMEM),
        compiler_params=pltpu.CompilerParams(vmem_limit_bytes=8 * MIB),
        name="codes",
    )(facts, swap(facts, 1))

    k_own = half(after(cached_keys, arrived), core, half_keys)
    first = []
    for some in sets:
        here = [block for _, block in some]
        if first:
            here[0] = after(here[0], first[-1])
        first.append(early_stats(here))
    if stepwise:
        off, block = final
        sets.append([final, (off ^ 1, swap(after(block, beside[2], code_own), 2))])
    else:
        sets.append([final])
    blocks = [block for some in sets for _, block in some]
    offsets = [off for some in sets for off, _ in some]
    late = [block for _, block in sets[-1]]
    count = len(offsets)
    per_block = GROUP * blocks[0].shape[0]
    sent = pl.pallas_call(
        functools.partial(stats_kernel, offsets, [x.shape[0] for x in first], chips),
        out_shape=jax.ShapeDtypeStruct((chips, count, HALF, per_block), jnp.float32),
        in_specs=[SMEM] + [VMEM] * (2 + len(first) + len(late)),
        out_specs=VMEM,
        scratch_shapes=[pltpu.VMEM((count, HALF, per_block), jnp.float32)],
        compiler_params=pltpu.CompilerParams(vmem_limit_bytes=8 * MIB),
        cost_estimate=score_cost(late),
        name="late_stats",
    )(place, k_own, k_sib, *first, *late)

    score_row = -(-2 * capacity // 16) * 16
    room = score_row + 8
    packed = pl.pallas_call(
        compact_kernel,
        out_shape=jax.ShapeDtypeStruct((peers, room, HEAD_DIM), jnp.bfloat16),
        in_specs=[SMEM, VMEM, VMEM, VMEM, ANYWHERE],
        out_specs=VMEM,
        scratch_shapes=[
            pltpu.VMEM(cached_values.shape, jnp.bfloat16),
            pltpu.VMEM((slots, 2 * HEAD_DIM), jnp.float32),
            pltpu.SemaphoreType.DMA,
        ],
        compiler_params=pltpu.CompilerParams(vmem_limit_bytes=GRANT),
        cost_estimate=pl.CostEstimate(
            flops=4 * slots * positions * KV_HEADS * HEAD_DIM,
            bytes_accessed=4 * positions * KV_HEADS * HEAD_DIM,
            transcendentals=0,
        ),
        name="compact",
    )(place, after(code_column, sent), k_own, k_other, cached_values)
    stats = lax.all_to_all(
        sent,
        "seq",
        split_axis=0,
        concat_axis=0,
        tiled=True,
        axis_index_groups=[[i for i in range(peers) if i % 2 == c] for c in range(2)],
    )
    factor = peers * positions / (GROUP * WINDOW * POOL)
    imp_own, imp_sib, sending = pl.pallas_call(
        functools.partial(mass_kernel, offsets, peers, factor, half_queries, len(edges), score_row),
        out_shape=(
            jax.ShapeDtypeStruct((HALF, positions), jnp.float32),
            jax.ShapeDtypeStruct((HALF, positions), jnp.float32),
            jax.ShapeDtypeStruct(packed.shape, packed.dtype),
        ),
        in_specs=[SMEM] + [VMEM] * (6 + len(edges) + count),
        out_specs=(VMEM, VMEM, VMEM),
        scratch_shapes=[
            pltpu.VMEM((count, HALF, per_block), jnp.float32),
            pltpu.VMEM((count * per_block, HEAD_DIM), jnp.float32),
        ],
        compiler_params=pltpu.CompilerParams(vmem_limit_bytes=12 * MIB),
        cost_estimate=score_cost(blocks),
        name="mass",
    )(place, stats, k_own, k_sib, code_own, code_sib, packed, *edges, *blocks)

    got = lax.all_to_all(sending, "seq", split_axis=0, concat_axis=0, tiled=True)
    by_core = got[:, score_row : score_row + 2, :capacity].reshape(chips, 2, 2, capacity)
    score_out = by_core[:, 0] + by_core[:, 1]
    got_rows = jnp.concatenate([got[:, :capacity], got[:, capacity : 2 * capacity]], axis=2)
    imp_other = swap(imp_sib, 1)
    importance = jnp.where(
        core == 0,
        jnp.concatenate([imp_own, imp_other], axis=0),
        jnp.concatenate([imp_other, imp_own], axis=0),
    )
    return (
        importance,
        got_rows.reshape(slots, 2 * HEAD_DIM),
        score_out.reshape(peers * capacity),
    )


def solution(mesh):
    in_specs = (
        P(("rep", "seq"), None),
        P(("rep", "seq"), None),
        P(("rep", "seq"), None),
        P(("rep", "seq")),
        P(("rep", "seq")),
        P(("rep", "seq")),
    )
    out_specs = (P("rep", "seq"), P(("rep", "seq"), None), P(("rep", "seq")))
    return jax.shard_map(
        per_device, mesh=mesh, in_specs=in_specs, out_specs=out_specs, check_vma=False
    )
```
